32 devices in a mesh: grp: 4 (over y, x), par: 8 (over z, core).
Axes of the slice: x: 2, y: 2, z: 4, core: 2. Of those that a mesh axis runs over, the one named last changes fastest.
Arguments:
- particles: float32 [16, 1048576], P('grp', 'par'), may hold values from -6 to 6
- scores: float32 [16, 1048576], P('grp', 'par'), may hold values from -6 to 6
- kernel_width: float32 [1], replicated, may hold values from 1 to 4
Outputs:
- drive: float32 [16, 1048576], P('grp', 'par')
- repel: float32 [16, 1048576], P('grp', 'par')
The draws below stay inside these ranges and needn't reach their ends.
All inputs are finite; a program needn't handle non-finite values.
Results may differ from the reference program's by a relative error of at most 0.000092.
Values sent between devices are 32-bit elements; how exact they have to be, the bound alone decides.
No kernel may reach another device: no remote copies, remote signals or barrier semaphores. Data moves between devices by JAX's collectives and lax.ppermute only.
A program may use at most 128 MiB of HBM per device.

```python
import math
import jax
import jax.numpy as jnp
from jax import lax

P_SIZE = 1048576
PARTICLES = 16


def draw_particles(key, part):
    key = jax.random.fold_in(key, 11)
    keys = jax.random.split(key, 4)
    center = jax.random.uniform(keys[0], (PARTICLES, 1), jnp.float32, -1.5, 1.5)
    spread = jax.random.uniform(keys[1], (PARTICLES, 1), jnp.float32, 0.3, 0.8)
    base = jax.random.normal(keys[2], (1, P_SIZE), jnp.float32)
    noise = jax.random.normal(keys[3], (PARTICLES, P_SIZE), jnp.float32)
    return jnp.clip(center * base + spread * noise, -6.0, 6.0)


def steps_of(key, shape, shards, low, top_value):
    def one(dim, shards_of):
        steps = jax.random.uniform(jax.random.fold_in(jax.random.fold_in(key, 6), dim), (shards_of,), jnp.float32, low / len(shards), top_value / len(shards))
        return jnp.repeat(jnp.exp(steps), shape[dim] // shards_of).reshape((-1,) + (1,) * (len(shape) - dim - 1))

    loudness = one(*shards[0])
    for cut in shards[1:]:
        loudness = loudness * one(*cut)
    return loudness


def centred(rng, dims, scale, limit, cuts=(), dtype=jnp.bfloat16):
    array = scale * jax.random.normal(rng, dims, jnp.float32)
    if cuts:
        array = array * steps_of(rng, dims, cuts, -0.22, 0.18)
    return jnp.clip(array, -limit, limit).astype(dtype)


def setup_inputs(seed: int = 0) -> dict:
    arg_keys = jax.random.split(jax.random.key(seed), 4)
    return {
        "particles": draw_particles(jax.random.fold_in(arg_keys[3], 71), 0),
        "scores": centred(arg_keys[1], (PARTICLES, P_SIZE), 1.0, 6.0, ((0, 4), (1, 8)), jnp.float32),
        "kernel_width": jnp.clip(jnp.exp(jax.random.uniform(arg_keys[2], (1,), jnp.float32, math.log(1.0), math.log(4.0))), 1.0, 4.0),
    }


def reference(particles, scores, kernel_width):
    highest = lax.Precision.HIGHEST
    norms = jnp.sum(particles * particles, axis=1)
    inner = lax.dot_general(particles, particles, (((1,), (1,)), ((), ())), precision=highest, preferred_element_type=jnp.float32)
    dist = norms[:, None] + norms[None, :] - 2.0 * inner
    kern = jnp.exp(-dist / (kernel_width[0] * P_SIZE))
    drive_sum = jnp.dot(kern, scores, precision=highest, preferred_element_type=jnp.float32)
    pull = jnp.dot(kern, particles, precision=highest, preferred_element_type=jnp.float32)
    weight = jnp.sum(kern, axis=1)
    drive = drive_sum / PARTICLES
    repel = (particles * weight[:, None] - pull) / (PARTICLES * kernel_width[0])
    return drive, repel
```

```python
import functools

import jax
import jax.numpy as jnp
from jax import lax
from jax.experimental import pallas as pl
from jax.experimental.pallas import tpu as pltpu
from jax.sharding import PartitionSpec as P

P_SIZE = 1048576
LANES = 128
SUB = 8
VMEM_LIMIT = 48 * 2**20

SMEM_SPEC = pl.BlockSpec(memory_space=pltpu.SMEM)
VMEM_SPEC = pl.BlockSpec(memory_space=pltpu.VMEM)


def dense(block):
    rows, columns = block.shape
    return block.reshape(rows, columns // LANES, LANES).transpose(1, 0, 2).reshape(-1, LANES)


def undense(block, rows):
    return block.reshape(-1, rows, LANES).transpose(1, 0, 2).reshape(rows, -1)


def gram_kernel(rows, groups, me_ref, *refs):
    xs, out_ref, acc_ref = refs[:groups], refs[groups], refs[groups + 1]
    me = me_ref[0]
    count = rows * groups
    step = SUB * rows
    steps = xs[0].shape[0] // step

    def load(ref, t, i):
        return ref[pl.ds(t * step + i, SUB, stride=rows), :]

    for a in range(groups):
        for b in range(a, groups):
            pairs = [(i, j) for i in range(rows) for j in range(rows) if a != b or i <= j]

            def body(t, sums):
                left = [load(xs[a], t, i) for i in range(rows)]
                right = left if a == b else [load(xs[b], t, j) for j in range(rows)]
                return tuple(s + left[i] * right[j] for s, (i, j) in zip(sums, pairs))

            zero = jnp.zeros((SUB, LANES), jnp.float32)
            sums = lax.fori_loop(0, steps, body, (zero,) * len(pairs), unroll=2)
            for s, (i, j) in zip(sums, pairs):
                row = jnp.sum(s, axis=0, keepdims=True)
                left, right = (me ^ a) * rows + i, (me ^ b) * rows + j
                acc_ref[pl.ds(left * count + right, 1), :] = row
                if a != b or i != j:
                    acc_ref[pl.ds(right * count + left, 1), :] = row
    total = lax.dot_general(
        jnp.ones((SUB, LANES), jnp.float32),
        acc_ref[...],
        (((1,), (1,)), ((), ())),
        precision=lax.Precision.HIGHEST,
        preferred_element_type=jnp.float32,
    )
    out_ref[...] = total[:1]


def gram(me, xs, rows):
    groups = len(xs)
    count = rows * groups
    return pl.pallas_call(
        functools.partial(gram_kernel, rows, groups),
        out_shape=jax.ShapeDtypeStruct((1, count * count), jnp.float32),
        in_specs=[SMEM_SPEC] + [VMEM_SPEC] * groups,
        out_specs=VMEM_SPEC,
        scratch_shapes=[pltpu.VMEM((count * count, LANES), jnp.float32)],
        compiler_params=pltpu.CompilerParams(vmem_limit_bytes=VMEM_LIMIT),
        name="gram",
    )(me, *xs)


def weights_kernel(width_ref, gram_ref, drive_ref, repel_ref):
    width = width_ref[0]
    inner = gram_ref[...]
    count = inner.shape[0]
    diagonal = lax.broadcasted_iota(jnp.int32, inner.shape, 0) == lax.broadcasted_iota(jnp.int32, inner.shape, 1)
    norms = jnp.where(diagonal, inner, 0.0)
    dist = jnp.sum(norms, axis=1, keepdims=True) + jnp.sum(norms, axis=0, keepdims=True) - 2.0 * inner
    kern = jnp.exp(-dist / (width * P_SIZE))
    others = jnp.where(diagonal, 0.0, kern)
    drive_ref[...] = kern / count
    repel_ref[...] = jnp.where(diagonal, jnp.sum(others, axis=1, keepdims=True), -others) / (count * width)


def weights(width, inner):
    shape = jax.ShapeDtypeStruct(inner.shape, jnp.float32)
    return pl.pallas_call(
        weights_kernel,
        out_shape=(shape, shape),
        in_specs=[SMEM_SPEC, VMEM_SPEC],
        out_specs=(VMEM_SPEC, VMEM_SPEC),
        name="weights",
    )(width, inner)


def mix_kernel(rows, groups, dest, me_ref, coef_ref, *refs):
    xs, out_ref, splat_ref = refs[:groups], refs[groups], refs[groups + 1]
    me = me_ref[0]
    count = rows * groups
    for i in range(rows):
        for b in range(groups):
            for j in range(rows):
                value = coef_ref[(me ^ dest) * rows + i, (me ^ b) * rows + j]
                splat_ref[i * count + b * rows + j] = jnp.full((SUB, LANES), value, jnp.float32)
    step = SUB * rows
    steps = xs[0].shape[0] // step
    wide = 2 if steps % 2 == 0 else 1

    def body(t, carry):
        base = t * step * wide
        sums = [[None] * rows for _ in range(wide)]
        for b in range(groups):
            for j in range(rows):
                x = [xs[b][pl.ds(base + u * step + j, SUB, stride=rows), :] for u in range(wide)]
                for i in range(rows):
                    c = splat_ref[i * count + b * rows + j]
                    for u in range(wide):
                        term = c * x[u]
                        sums[u][i] = term if sums[u][i] is None else sums[u][i] + term
        for u in range(wide):
            for i in range(rows):
                out_ref[pl.ds(base + u * step + i, SUB, stride=rows), :] = sums[u][i]
        return carry

    lax.fori_loop(0, steps // wide, body, 0)


def mix(me, coef, xs, rows, dest, whole=False):
    groups = len(xs)
    count = rows * groups
    part = xs[0].shape
    return pl.pallas_call(
        functools.partial(mix_kernel, rows, groups, dest),
        out_shape=jax.ShapeDtypeStruct((part[0] * groups, LANES) if whole else part, jnp.float32),
        grid_spec=pltpu.PrefetchScalarGridSpec(
            num_scalar_prefetch=1,
            grid=(1,),
            in_specs=[SMEM_SPEC] + [pl.BlockSpec(part, lambda t, me: (0, 0))] * groups,
            out_specs=pl.BlockSpec(part, lambda t, me: (me[0] if whole else 0, 0)),
            scratch_shapes=[pltpu.VMEM((rows * count, SUB, LANES), jnp.float32)],
        ),
        compiler_params=pltpu.CompilerParams(vmem_limit_bytes=VMEM_LIMIT),
        name="mix",
    )(me, coef, *xs)


def shards(particles, scores, kernel_width):
    groups = lax.axis_size("grp")
    rows = particles.shape[0]
    count = rows * groups
    me = lax.axis_index("grp")
    place = me.astype(jnp.int32).reshape(1)
    x, s = dense(particles), dense(scores)
    part = x.shape[0] // groups

    def swap(block, k):
        return lax.ppermute(block, "grp", [(i, i ^ k) for i in range(groups)])

    def cut(block, k):
        return lax.dynamic_slice_in_dim(block, (me ^ k) * part, part, axis=0)

    def spread(block):
        return [cut(block, 0)] + [swap(cut(block, k), k) for k in range(1, groups)]

    xs = spread(x)
    xs, s = lax.optimization_barrier((xs, s))
    ss = spread(s)
    inner = lax.psum(gram(place, xs, rows), ("grp", "par")).reshape(count, count)
    to_drive, to_repel = weights(kernel_width, inner)

    def collect(coef, parts):
        back = [swap(mix(place, coef, parts, rows, k), k) for k in range(1, groups)]
        out = mix(place, coef, parts, rows, 0, whole=True)
        for k, block in enumerate(back, 1):
            out = lax.dynamic_update_slice_in_dim(out, block, (me ^ k) * part, axis=0)
        return undense(out, rows)

    repel = collect(to_repel, xs)
    drive = collect(to_drive, ss)
    return (drive, repel)


def solution(mesh):
    return jax.shard_map(
        shards,
        mesh=mesh,
        in_specs=(P("grp", "par"), P("grp", "par"), P()),
        out_specs=(P("grp", "par"), P("grp", "par")),
        check_vma=False,
    )
```

```python
import functools

import jax
import jax.numpy as jnp
from jax import lax
from jax.experimental import pallas as pl
from jax.experimental.pallas import tpu as pltpu
from jax.sharding import PartitionSpec as P

P_SIZE = 1048576
LANES = 128
SUB = 8
VMEM_LIMIT = 16 * 2**20

SMEM_SPEC = pl.BlockSpec(memory_space=pltpu.SMEM)
VMEM_SPEC = pl.BlockSpec(memory_space=pltpu.VMEM)
HBM_SPEC = pl.BlockSpec(memory_space=pltpu.HBM)
SHORT = pl.CostEstimate(flops=1, bytes_accessed=1, transcendentals=0)


def dense(block):
    rows, columns = block.shape
    return block.reshape(rows, columns // LANES, LANES).transpose(1, 0, 2).reshape(-1, LANES)


def undense(block, rows):
    return block.reshape(-1, rows, LANES).transpose(1, 0, 2).reshape(rows, -1)


def gram_kernel(rows, groups, me_ref, *refs):
    xs, out_ref, acc_ref = refs[:groups], refs[groups], refs[groups + 1]
    me = me_ref[0]
    count = rows * groups
    step = SUB * rows
    steps = xs[0].shape[0] // step

    def load(ref, t, i):
        return ref[pl.ds(t * step + i, SUB, stride=rows), :]

    for a in range(groups):
        for b in range(a, groups):
            pairs = [(i, j) for i in range(rows) for j in range(rows) if a != b or i <= j]

            def body(t, sums):
                left = [load(xs[a], t, i) for i in range(rows)]
                right = left if a == b else [load(xs[b], t, j) for j in range(rows)]
                return tuple(s + left[i] * right[j] for s, (i, j) in zip(sums, pairs))

            zero = jnp.zeros((SUB, LANES), jnp.float32)
            sums = lax.fori_loop(0, steps, body, (zero,) * len(pairs), unroll=2)
            for s, (i, j) in zip(sums, pairs):
                row = jnp.sum(s, axis=0, keepdims=True)
                left, right = (me ^ a) * rows + i, (me ^ b) * rows + j
                acc_ref[pl.ds(left * count + right, 1), :] = row
                if a != b or i != j:
                    acc_ref[pl.ds(right * count + left, 1), :] = row
    total = lax.dot_general(
        jnp.ones((SUB, LANES), jnp.float32),
        acc_ref[...],
        (((1,), (1,)), ((), ())),
        precision=lax.Precision.HIGHEST,
        preferred_element_type=jnp.float32,
    )
    for n in range(count * count // LANES):
        row = total[:1, n * LANES : (n + 1) * LANES]
        out_ref[:, n : n + 1, :] = jnp.broadcast_to(row[None], (out_ref.shape[0], 1, LANES))


def gram(me, xs, rows, copies):
    groups = len(xs)
    count = rows * groups
    return pl.pallas_call(
        functools.partial(gram_kernel, rows, groups),
        out_shape=jax.ShapeDtypeStruct((copies, count * count // LANES, LANES), jnp.float32),
        in_specs=[SMEM_SPEC] + [VMEM_SPEC] * groups,
        out_specs=VMEM_SPEC,
        scratch_shapes=[pltpu.VMEM((count * count, LANES), jnp.float32)],
        compiler_params=pltpu.CompilerParams(vmem_limit_bytes=VMEM_LIMIT),
        cost_estimate=SHORT,
        name="gram",
    )(me, *xs)


def relay_kernel(grams_ref, token_ref, out_ref):
    total = jnp.sum(grams_ref[...], axis=0, keepdims=True)
    out_ref[...] = jnp.broadcast_to(total, out_ref.shape)


def relay(grams, token, copies):
    return pl.pallas_call(
        relay_kernel,
        out_shape=jax.ShapeDtypeStruct((copies, *grams.shape[1:]), jnp.float32),
        in_specs=[VMEM_SPEC, VMEM_SPEC],
        out_specs=VMEM_SPEC,
        compiler_params=pltpu.CompilerParams(vmem_limit_bytes=2**21),
        cost_estimate=SHORT,
        name="relay",
    )(grams, token)


def exact(left, right):
    return jnp.dot(left, right, precision=lax.Precision.HIGHEST, preferred_element_type=jnp.float32)


def weights_kernel(rows, count, me_ref, width_ref, grams_ref, drive_ref, repel_ref):
    def iota(shape, axis):
        return lax.broadcasted_iota(jnp.int32, shape, axis)

    def mask(condition):
        return jnp.where(condition, 1.0, 0.0)

    flat = jnp.sum(grams_ref[...], axis=0)
    lines = flat.shape[0]
    per = LANES // count
    held = exact(mask(iota((count, lines), 0) // per == iota((count, lines), 1)), flat)
    held = jnp.where(iota((count, LANES), 1) // count == iota((count, LANES), 0) % per, held, 0.0)
    inner = exact(held, mask(iota((LANES, count), 0) % count == iota((LANES, count), 1)))
    square = (count, count)
    r, c = iota(square, 0), iota(square, 1)
    order = mask(((me_ref[0] ^ (r // rows)) * rows + r % rows) == c)
    inner = exact(exact(order, inner), order)

    width = width_ref[0]
    diagonal = r == c
    norms = jnp.where(diagonal, inner, 0.0)
    dist = jnp.sum(norms, axis=1, keepdims=True) + jnp.sum(norms, axis=0, keepdims=True) - 2.0 * inner
    kern = jnp.exp(-dist / (width * P_SIZE))
    others = jnp.where(diagonal, 0.0, kern)
    to_drive = kern / count
    to_repel = jnp.where(diagonal, jnp.sum(others, axis=1, keepdims=True), -others) / (count * width)
    for j in range(count):
        drive_ref[j * count : (j + 1) * count, :] = jnp.broadcast_to(to_drive[:, j : j + 1], (count, LANES))
        repel_ref[j * count : (j + 1) * count, :] = jnp.broadcast_to(to_repel[:, j : j + 1], (count, LANES))


def weights(me, width, grams, rows, count):
    shape = jax.ShapeDtypeStruct((count * count, LANES), jnp.float32)
    return pl.pallas_call(
        functools.partial(weights_kernel, rows, count),
        out_shape=(shape, shape),
        in_specs=[SMEM_SPEC, SMEM_SPEC, VMEM_SPEC],
        out_specs=(VMEM_SPEC, VMEM_SPEC),
        compiler_params=pltpu.CompilerParams(vmem_limit_bytes=VMEM_LIMIT),
        cost_estimate=SHORT,
        name="weights",
    )(me, width, grams)


def mix_kernel(rows, count, jobs, drive_ref, repel_ref, *refs):
    out_ref = refs[-1]
    step = SUB * rows
    start = used = 0
    for coef_ref, dest, sources in ((repel_ref if repel else drive_ref, dest, sources) for repel, dest, sources in jobs):
        xs = refs[used : used + len(sources)]
        used += len(sources)
        steps = xs[0].shape[0] // step
        wide = next(w for w in (8, 4, 2, 1) if steps % w == 0)

        def body(t, carry):
            base = pl.multiple_of(t * step * wide, step)
            sums = [[None] * rows for _ in range(wide)]
            for b, source in enumerate(sources):
                for j in range(rows):
                    x = [xs[b][pl.ds(base + u * step + j, SUB, stride=rows), :] for u in range(wide)]
                    for i in range(rows):
                        row = (source * rows + j) * count + dest * rows + i
                        c = jnp.broadcast_to(coef_ref[row : row + 1, :], (SUB, LANES))
                        for u in range(wide):
                            term = c * x[u]
                            sums[u][i] = term if sums[u][i] is None else sums[u][i] + term
            for u in range(wide):
                for i in range(rows):
                    out_ref[pl.ds(start + base + u * step + i, SUB, stride=rows), :] = sums[u][i]
            return carry

        lax.fori_loop(0, steps // wide, body, 0)
        start += steps * step


def mix(coefs, rows, count, jobs, tokens=()):
    blocks = [block for job in jobs for block in job[3]]
    size = sum(job[3][0].shape[0] for job in jobs)
    return pl.pallas_call(
        functools.partial(mix_kernel, rows, count, [job[:3] for job in jobs]),
        out_shape=jax.ShapeDtypeStruct((size, LANES), jnp.float32),
        in_specs=[VMEM_SPEC] * (2 + len(blocks) + len(tokens)),
        out_specs=VMEM_SPEC,
        compiler_params=pltpu.CompilerParams(vmem_limit_bytes=VMEM_LIMIT),
        cost_estimate=SHORT,
        name="mix",
    )(*coefs, *blocks, *tokens)


def put_kernel(entries, blocks, me_ref, *refs):
    blocks, (out_ref, sum_ref, sems) = refs[:blocks], refs[-3:]
    copies = []
    used = 0
    for n, (parts, size, place) in enumerate(entries):
        block, start = parts[0]
        source = blocks[block].at[pl.ds(start, size), :]
        if len(parts) > 1:
            total = source[...]
            for block, start in parts[1:]:
                total = total + blocks[block][pl.ds(start, size), :]
            source = sum_ref.at[pl.ds(used, size), :]
            source[...] = total
            used += size
        offset = place[1] if place[0] else (me_ref[0] ^ place[1]) * size
        copy = pltpu.make_async_copy(source, out_ref.at[pl.ds(offset, size), :], sems.at[n])
        copy.start()
        copies.append(copy)
    for copy in copies:
        copy.wait()


def put(me, entries, blocks, size, base=None):
    extra = [] if base is None else [base]
    moved = sum(entry[1] for entry in entries)
    scratch = sum(entry[1] for entry in entries if len(entry[0]) > 1)
    return pl.pallas_call(
        functools.partial(put_kernel, entries, len(blocks)),
        out_shape=jax.ShapeDtypeStruct((size, LANES), jnp.float32),
        in_specs=[SMEM_SPEC] + [VMEM_SPEC] * len(blocks) + [HBM_SPEC] * len(extra),
        out_specs=HBM_SPEC,
        scratch_shapes=[pltpu.VMEM((max(scratch, SUB), LANES), jnp.float32), pltpu.SemaphoreType.DMA((len(entries),))],
        input_output_aliases={1 + len(blocks): 0} if extra else {},
        compiler_params=pltpu.CompilerParams(vmem_limit_bytes=VMEM_LIMIT),
        cost_estimate=pl.CostEstimate(flops=0, bytes_accessed=8 * LANES * moved, transcendentals=0),
        name="put",
    )(me, *blocks, *extra)


def cut_kernel(places, me_ref, block_ref, *refs):
    outs, sems = refs[:-1], refs[-1]
    size = outs[0].shape[0]
    copies = [
        pltpu.make_async_copy(block_ref.at[pl.ds((me_ref[0] ^ place) * size, size), :], out, sems.at[n])
        for n, (out, place) in enumerate(zip(outs, places))
    ]
    for copy in copies:
        copy.start()
    for copy in copies:
        copy.wait()


def cut(me, block, places, groups):
    part = jax.ShapeDtypeStruct((block.shape[0] // groups, LANES), jnp.float32)
    return pl.pallas_call(
        functools.partial(cut_kernel, places),
        out_shape=[part] * len(places),
        in_specs=[SMEM_SPEC, HBM_SPEC],
        out_specs=[VMEM_SPEC] * len(places),
        scratch_shapes=[pltpu.SemaphoreType.DMA((len(places),))],
        compiler_params=pltpu.CompilerParams(vmem_limit_bytes=60 * 2**20),
        cost_estimate=SHORT,
        name="cut",
    )(me, block)


def arrived_kernel(*refs):
    refs[-1][...] = jnp.zeros_like(refs[-1])


def arrived(blocks):
    return pl.pallas_call(
        arrived_kernel,
        out_shape=jax.ShapeDtypeStruct((SUB, LANES), jnp.float32),
        in_specs=[pl.BlockSpec(memory_space=pl.ANY)] * len(blocks),
        out_specs=VMEM_SPEC,
        compiler_params=pltpu.CompilerParams(vmem_limit_bytes=2**21),
        cost_estimate=pl.CostEstimate(flops=0, bytes_accessed=10**9, transcendentals=0),
        name="arrived",
    )(*blocks)


def shards(particles, scores, kernel_width):
    groups = lax.axis_size("grp")
    rows = particles.shape[0]
    count = rows * groups
    me = lax.axis_index("grp")
    place = me.astype(jnp.int32).reshape(1)
    x, s = dense(particles), dense(scores)
    part, half = x.shape[0] // groups, x.shape[0] // 2
    near = 2 ** ((groups.bit_length() - 1) // 2)
    lows, highs = list(range(near)), list(range(0, groups, near))

    def swap(block, k):
        return lax.ppermute(block, "grp", [(i, i ^ k) for i in range(groups)]) if k else block

    everyone, others = list(range(groups)), list(range(groups - 1, 0, -1))
    size, step = x.shape[0], SUB * rows
    first = max(1, half // step * 5 // 16) * step
    second = half - first

    sent = cut(place, x, others, groups)
    (x, s), sent = lax.optimization_barrier(((x, s), sent))
    s_own = [s[:first], s[first:half], s[half : half + first], s[half + first :]]
    xs = {k: swap(block, k) for k, block in zip(others, sent)}
    xs[0] = lax.dynamic_slice_in_dim(x, me * part, part, axis=0)
    xs = [xs[k] for k in everyone]

    def exchange(low, high):
        return [swap(low, k) for k in lows], [swap(high, k) for k in highs]

    def gather(grams, axis):
        return lax.all_to_all(grams, axis, 0, 0, tiled=True)

    xs, s_own = lax.optimization_barrier((xs, s_own))
    early = exchange(s_own[0], s_own[2])
    grams = gather(gram(place, xs, rows, groups), "grp")
    early, pair, grams = lax.optimization_barrier((early, (s_own[1], s_own[3]), grams))
    late = exchange(*pair)
    grams = gather(relay(grams, arrived(early[0][1:] + early[1][1:]), lax.axis_size("par")), "par")
    coefs = weights(place, kernel_width, grams, rows, count)
    token = arrived(late[0][1:] + late[1][1:])

    def send(dest, jobs, coefs, tokens=()):
        mixed = mix(coefs, rows, count, jobs, tokens)
        return swap(mixed, dest), lax.optimization_barrier((coefs, mixed))[0]

    def score_jobs(dest, sources, n):
        return [(False, dest, sources, early[n]), (False, dest, sources, late[n])]

    back, sums = {}, {}
    for n, (sources, dests) in enumerate(((lows, highs), (highs, lows))):
        for k in dests[1:]:
            sums[k], coefs = send(k, score_jobs(k, sources, n), coefs, [token])
    for k in others:
        back[k], coefs = send(k, [(True, k, everyone, xs)], coefs)
    own = mix(coefs, rows, count, [(True, 0, everyone, xs)] + score_jobs(0, lows, 0) + score_jobs(0, highs, 1))

    repel = put(place, [([(0, 0)], part, (False, 0))], [own], size)
    drive = None
    for n, dests in enumerate((highs[1:], lows[1:])):
        got = [sums[k] for k in dests]
        if drive is not None:
            drive, got = lax.optimization_barrier((drive, got))
        parts = [(0, part + n * half)] + [(1 + m, 0) for m in range(len(got))]
        drive = put(place, [(parts, half, (True, n * half))], [own] + got, size, base=drive)
    for dests in (others[:1], others[1:]):
        if dests:
            got = [back[k] for k in dests]
            (drive, repel), got = lax.optimization_barrier(((drive, repel), got))
            repel = put(place, [([(m, 0)], part, (False, k)) for m, k in enumerate(dests)], got, size, base=repel)
    return (undense(drive, rows), undense(repel, rows))


def solution(mesh):
    return jax.shard_map(
        shards,
        mesh=mesh,
        in_specs=(P("grp", "par"), P("grp", "par"), P()),
        out_specs=(P("grp", "par"), P("grp", "par")),
        check_vma=False,
    )
```

```python
import functools

import jax
import jax.numpy as jnp
from jax import lax
from jax.experimental import pallas as pl
from jax.experimental.pallas import tpu as pltpu
from jax.sharding import PartitionSpec as P

P_SIZE = 1048576
LANES = 128
SUB = 8
VMEM_LIMIT = 16 * 2**20

SMEM_SPEC = pl.BlockSpec(memory_space=pltpu.SMEM)
VMEM_SPEC = pl.BlockSpec(memory_space=pltpu.VMEM)
ANY_SPEC = pl.BlockSpec(memory_space=pl.ANY)
HBM_SPEC = pl.BlockSpec(memory_space=pltpu.HBM)
SHORT = pl.CostEstimate(flops=1, bytes_accessed=1, transcendentals=0)


def dense(block):
    rows, columns = block.shape
    return block.reshape(rows, columns // LANES, LANES).transpose(1, 0, 2).reshape(-1, LANES)


def undense(block, rows):
    return block.reshape(-1, rows, LANES).transpose(1, 0, 2).reshape(rows, -1)


def gram_kernel(rows, groups, me_ref, *refs):
    xs, out_ref, acc_ref = refs[:groups], refs[groups], refs[groups + 1]
    me = me_ref[0]
    count = rows * groups
    step = SUB * rows
    steps = xs[0].shape[0] // step

    def load(ref, t, i):
        return ref[pl.ds(t * step + i, SUB, stride=rows), :]

    for a in range(groups):
        for b in range(a, groups):
            pairs = [(i, j) for i in range(rows) for j in range(rows) if a != b or i <= j]

            def body(t, sums):
                left = [load(xs[a], t, i) for i in range(rows)]
                right = left if a == b else [load(xs[b], t, j) for j in range(rows)]
                return tuple(s + left[i] * right[j] for s, (i, j) in zip(sums, pairs))

            zero = jnp.zeros((SUB, LANES), jnp.float32)
            sums = lax.fori_loop(0, steps, body, (zero,) * len(pairs), unroll=2)
            for s, (i, j) in zip(sums, pairs):
                row = jnp.sum(s, axis=0, keepdims=True)
                left, right = (me ^ a) * rows + i, (me ^ b) * rows + j
                acc_ref[pl.ds(left * count + right, 1), :] = row
                if a != b or i != j:
                    acc_ref[pl.ds(right * count + left, 1), :] = row
    total = lax.dot_general(
        jnp.ones((SUB, LANES), jnp.float32),
        acc_ref[...],
        (((1,), (1,)), ((), ())),
        precision=lax.Precision.HIGHEST,
        preferred_element_type=jnp.float32,
    )
    for n in range(count * count // LANES):
        row = total[:1, n * LANES : (n + 1) * LANES]
        out_ref[:, n : n + 1, :] = jnp.broadcast_to(row[None], (out_ref.shape[0], 1, LANES))


def gram(me, xs, rows, copies):
    groups = len(xs)
    count = rows * groups
    return pl.pallas_call(
        functools.partial(gram_kernel, rows, groups),
        out_shape=jax.ShapeDtypeStruct((copies, count * count // LANES, LANES), jnp.float32),
        in_specs=[SMEM_SPEC] + [VMEM_SPEC] * groups,
        out_specs=VMEM_SPEC,
        scratch_shapes=[pltpu.VMEM((count * count, LANES), jnp.float32)],
        compiler_params=pltpu.CompilerParams(vmem_limit_bytes=VMEM_LIMIT),
        cost_estimate=SHORT,
        name="gram",
    )(me, *xs)


def exact(left, right):
    return jnp.dot(left, right, precision=lax.Precision.HIGHEST, preferred_element_type=jnp.float32)


def weights_kernel(rows, count, me_ref, width_ref, grams_ref, drive_ref, repel_ref):
    def iota(shape, axis):
        return lax.broadcasted_iota(jnp.int32, shape, axis)

    def mask(condition):
        return jnp.where(condition, 1.0, 0.0)

    flat = jnp.sum(grams_ref[...], axis=0)
    lines = flat.shape[0]
    per = LANES // count
    held = exact(mask(iota((count, lines), 0) // per == iota((count, lines), 1)), flat)
    held = jnp.where(iota((count, LANES), 1) // count == iota((count, LANES), 0) % per, held, 0.0)
    inner = exact(held, mask(iota((LANES, count), 0) % count == iota((LANES, count), 1)))
    square = (count, count)
    r, c = iota(square, 0), iota(square, 1)
    order = mask(((me_ref[0] ^ (r // rows)) * rows + r % rows) == c)
    inner = exact(exact(order, inner), order)

    width = width_ref[0]
    diagonal = r == c
    norms = jnp.where(diagonal, inner, 0.0)
    dist = jnp.sum(norms, axis=1, keepdims=True) + jnp.sum(norms, axis=0, keepdims=True) - 2.0 * inner
    kern = jnp.exp(-dist / (width * P_SIZE))
    others = jnp.where(diagonal, 0.0, kern)
    to_drive = kern / count
    to_repel = jnp.where(diagonal, jnp.sum(others, axis=1, keepdims=True), -others) / (count * width)
    for j in range(count):
        drive_ref[j * count : (j + 1) * count, :] = jnp.broadcast_to(to_drive[:, j : j + 1], (count, LANES))
        repel_ref[j * count : (j + 1) * count, :] = jnp.broadcast_to(to_repel[:, j : j + 1], (count, LANES))


def weights(me, width, grams, rows, count):
    shape = jax.ShapeDtypeStruct((count * count, LANES), jnp.float32)
    return pl.pallas_call(
        functools.partial(weights_kernel, rows, count),
        out_shape=(shape, shape),
        in_specs=[SMEM_SPEC, SMEM_SPEC, VMEM_SPEC],
        out_specs=(VMEM_SPEC, VMEM_SPEC),
        compiler_params=pltpu.CompilerParams(vmem_limit_bytes=VMEM_LIMIT),
        cost_estimate=SHORT,
        name="weights",
    )(me, width, grams)


def mix_kernel(rows, count, jobs, drive_ref, repel_ref, *refs):
    blocks = sum(len(spans) for _, _, _, spans in jobs)
    xs, out_ref, scratch = list(refs[:blocks]), refs[blocks], refs[blocks + 1 :]
    streams = [n for n, span in enumerate(span for job in jobs for span in job[3]) if span is not None]
    spans = [span for job in jobs for span in job[3]]
    copies = {}
    for m, n in enumerate(streams):
        start, size = spans[n]
        copies[n] = pltpu.make_async_copy(xs[n].at[pl.ds(start, size), :], scratch[m], scratch[-1].at[m])
        copies[n].start()
        xs[n] = scratch[m]
    step = SUB * rows
    start = used = 0
    for repel, dest, sources, spans in jobs:
        coef_ref = repel_ref if repel else drive_ref
        held = xs[used : used + len(sources)]
        for n in range(used, used + len(sources)):
            if n in copies:
                copies[n].wait()
        used += len(sources)
        steps = held[0].shape[0] // step
        wide = next(w for w in (8, 4, 2, 1) if steps % w == 0)

        def body(t, carry):
            base = pl.multiple_of(t * step * wide, step)
            sums = [[None] * rows for _ in range(wide)]
            for b, source in enumerate(sources):
                for j in range(rows):
                    x = [held[b][pl.ds(base + u * step + j, SUB, stride=rows), :] for u in range(wide)]
                    for i in range(rows):
                        row = (source * rows + j) * count + dest * rows + i
                        c = jnp.broadcast_to(coef_ref[row : row + 1, :], (SUB, LANES))
                        for u in range(wide):
                            term = c * x[u]
                            sums[u][i] = term if sums[u][i] is None else sums[u][i] + term
            for u in range(wide):
                for i in range(rows):
                    out_ref[pl.ds(start + base + u * step + i, SUB, stride=rows), :] = sums[u][i]
            return carry

        lax.fori_loop(0, steps // wide, body, 0)
        start += steps * step


def mix(coefs, rows, count, jobs):
    blocks = [block for job in jobs for block in job[3]]
    streams = [block for block in blocks if isinstance(block, tuple)]
    spans = [(*job[:3], [b[1:] if isinstance(b, tuple) else None for b in job[3]]) for job in jobs]
    size = sum(b[2] if isinstance(b, tuple) else b.shape[0] for b in (job[3][0] for job in jobs))
    scratch = [pltpu.VMEM((block[2], LANES), jnp.float32) for block in streams]
    return pl.pallas_call(
        functools.partial(mix_kernel, rows, count, spans),
        out_shape=jax.ShapeDtypeStruct((size, LANES), jnp.float32),
        in_specs=[VMEM_SPEC] * 2 + [ANY_SPEC if isinstance(block, tuple) else VMEM_SPEC for block in blocks],
        out_specs=VMEM_SPEC,
        scratch_shapes=scratch + ([pltpu.SemaphoreType.DMA((len(streams),))] if streams else []),
        compiler_params=pltpu.CompilerParams(vmem_limit_bytes=VMEM_LIMIT),
        cost_estimate=SHORT,
        name="mix",
    )(*coefs, *[block[0] if isinstance(block, tuple) else block for block in blocks])


def put_kernel(entries, blocks, me_ref, *refs):
    blocks, (out_ref, sum_ref, sems) = refs[:blocks], refs[-3:]
    copies = []
    used = 0
    for n, (parts, size, place) in enumerate(entries):
        block, start = parts[0]
        source = blocks[block].at[pl.ds(start, size), :]
        if len(parts) > 1:
            total = source[...]
            for block, start in parts[1:]:
                total = total + blocks[block][pl.ds(start, size), :]
            source = sum_ref.at[pl.ds(used, size), :]
            source[...] = total
            used += size
        offset = place[1] if place[0] else (me_ref[0] ^ place[1]) * size
        copy = pltpu.make_async_copy(source, out_ref.at[pl.ds(offset, size), :], sems.at[n])
        copy.start()
        copies.append(copy)
    for copy in copies:
        copy.wait()


def put(me, entries, blocks, size, base=None):
    extra = [] if base is None else [base]
    moved = sum(entry[1] for entry in entries)
    scratch = sum(entry[1] for entry in entries if len(entry[0]) > 1)
    return pl.pallas_call(
        functools.partial(put_kernel, entries, len(blocks)),
        out_shape=jax.ShapeDtypeStruct((size, LANES), jnp.float32),
        in_specs=[SMEM_SPEC] + [VMEM_SPEC] * len(blocks) + [HBM_SPEC] * len(extra),
        out_specs=HBM_SPEC,
        scratch_shapes=[pltpu.VMEM((max(scratch, SUB), LANES), jnp.float32), pltpu.SemaphoreType.DMA((len(entries),))],
        input_output_aliases={1 + len(blocks): 0} if extra else {},
        compiler_params=pltpu.CompilerParams(vmem_limit_bytes=VMEM_LIMIT),
        cost_estimate=pl.CostEstimate(flops=0, bytes_accessed=8 * LANES * moved, transcendentals=0),
        name="put",
    )(me, *blocks, *extra)


def shards(particles, scores, kernel_width):
    groups = lax.axis_size("grp")
    rows = particles.shape[0]
    count = rows * groups
    me = lax.axis_index("grp")
    place = me.astype(jnp.int32).reshape(1)
    x, s = dense(particles), dense(scores)
    part, half = x.shape[0] // groups, x.shape[0] // 2
    near = 2 ** ((groups.bit_length() - 1) // 2)
    lows, highs = list(range(near)), list(range(0, groups, near))

    def swap(block, k):
        return lax.ppermute(block, "grp", [(i, i ^ k) for i in range(groups)]) if k else block

    everyone, others = list(range(groups)), list(range(groups - 1, 0, -1))
    size, step = x.shape[0], SUB * rows
    first = max(1, half // step * 3 // 8) * step
    second = half - first

    def cut(block, k):
        return lax.dynamic_slice_in_dim(block, (me ^ k) * part, part, axis=0)

    sent = [cut(x, k) for k in others + [0]]
    s, sent = lax.optimization_barrier((s, sent))
    s_own = [s[:first], s[first:half], s[half : half + first], s[half + first :]]
    xs = {k: swap(block, k) for k, block in zip(others + [0], sent)}
    xs = [xs[k] for k in everyone]

    def exchange(low, high):
        return [swap(low, k) for k in lows], [swap(high, k) for k in highs]

    xs[-1], s_own = lax.optimization_barrier((xs[-1], s_own))
    early = exchange(s_own[0], s_own[2])
    inner = gram(place, xs, rows, 1)
    grams = [swap(inner, k) for k in everyone]
    early, pair, grams = lax.optimization_barrier((early, (s_own[1], s_own[3]), grams))
    late = exchange(*pair)
    coefs = weights(place, kernel_width, lax.psum(sum(grams[1:], grams[0]), "par"), rows, count)

    def send(dest, jobs, coefs):
        mixed = mix(coefs, rows, count, jobs)
        return swap(mixed, dest), lax.optimization_barrier((coefs, mixed))[0]

    def score_job(dest, n, held, start, size):
        own = (s, n * half + start, size)
        return (False, dest, (lows, highs)[n], [own] + [(block, 0, size) for block in held[n][1:]])

    near_by = [k for k in others if k in lows or k in highs]
    back, sums = {}, {}
    for k in near_by + [k for k in others if k not in near_by]:
        back[k], coefs = send(k, [(True, k, everyone, xs)], coefs)
    pieces = ((late, first, second), (early, 0, first))
    for p, piece in enumerate(pieces):
        for n, dests in enumerate((highs[1:], lows[1:])):
            for k in dests:
                sums[p, k], coefs = send(k, [score_job(k, n, *piece)], coefs)
    own = mix(coefs, rows, count, [(True, 0, everyone, xs)] + [score_job(0, n, *piece) for piece in pieces for n in (0, 1)])

    repel = put(place, [([(0, 0)], part, (False, 0))], [own], size)
    for k in back:
        repel, back[k] = lax.optimization_barrier((repel, back[k]))
        repel = put(place, [([(0, 0)], part, (False, k))], [back[k]], size, base=repel)
    drive = None
    begin = part
    for p, (held, row, length) in enumerate(pieces):
        entries, blocks = [], [own]
        for n, dests in enumerate((highs[1:], lows[1:])):
            entries.append(([(0, begin)] + [(len(blocks) + m, 0) for m in range(len(dests))], length, (True, n * half + row)))
            blocks += [sums[p, k] for k in dests]
            begin += length
        held = repel if drive is None else (drive, repel)
        held, blocks = lax.optimization_barrier((held, blocks))
        drive, repel = (None, held) if drive is None else held
        drive = put(place, entries, blocks, size, base=drive)
    return (undense(drive, rows), undense(repel, rows))


def solution(mesh):
    return jax.shard_map(
        shards,
        mesh=mesh,
        in_specs=(P("grp", "par"), P("grp", "par"), P()),
        out_specs=(P("grp", "par"), P("grp", "par")),
        check_vma=False,
    )
```

```python
import functools

import jax
import jax.numpy as jnp
from jax import lax
from jax.experimental import pallas as pl
from jax.experimental.pallas import tpu as pltpu
from jax.sharding import PartitionSpec as P

P_SIZE = 1048576
LANES = 128
SUB = 8
VMEM_LIMIT = 16 * 2**20

SMEM_SPEC = pl.BlockSpec(memory_space=pltpu.SMEM)
VMEM_SPEC = pl.BlockSpec(memory_space=pltpu.VMEM)
ANY_SPEC = pl.BlockSpec(memory_space=pl.ANY)
HBM_SPEC = pl.BlockSpec(memory_space=pltpu.HBM)
SHORT = pl.CostEstimate(flops=1, bytes_accessed=1, transcendentals=0)


def in_hbm(array):
    return pltpu.with_memory_space_constraint(array, pltpu.HBM)


def in_vmem(array):
    return pltpu.with_memory_space_constraint(array, pltpu.VMEM)


def dense(block):
    rows, columns = block.shape
    return block.reshape(rows, columns // LANES, LANES).transpose(1, 0, 2).reshape(-1, LANES)


def undense(block, rows):
    return block.reshape(-1, rows, LANES).transpose(1, 0, 2).reshape(rows, -1)


def gram_kernel(rows, groups, me_ref, *refs):
    xs, out_ref, acc_ref = refs[:groups], refs[groups], refs[groups + 1]
    me = me_ref[0]
    count = rows * groups
    step = SUB * rows
    steps = xs[0].shape[0] // step

    def load(ref, t, i):
        return ref[pl.ds(t * step + i, SUB, stride=rows), :]

    for a in range(groups):
        for b in range(a, groups):
            pairs = [(i, j) for i in range(rows) for j in range(rows) if a != b or i <= j]

            def body(t, sums):
                left = [load(xs[a], t, i) for i in range(rows)]
                right = left if a == b else [load(xs[b], t, j) for j in range(rows)]
                return tuple(s + left[i] * right[j] for s, (i, j) in zip(sums, pairs))

            zero = jnp.zeros((SUB, LANES), jnp.float32)
            sums = lax.fori_loop(0, steps, body, (zero,) * len(pairs), unroll=2)
            for s, (i, j) in zip(sums, pairs):
                row = jnp.sum(s, axis=0, keepdims=True)
                left, right = (me ^ a) * rows + i, (me ^ b) * rows + j
                acc_ref[pl.ds(left * count + right, 1), :] = row
                if a != b or i != j:
                    acc_ref[pl.ds(right * count + left, 1), :] = row
    total = lax.dot_general(
        jnp.ones((SUB, LANES), jnp.float32),
        acc_ref[...],
        (((1,), (1,)), ((), ())),
        precision=lax.Precision.HIGHEST,
        preferred_element_type=jnp.float32,
    )
    for n in range(count * count // LANES):
        row = total[:1, n * LANES : (n + 1) * LANES]
        out_ref[:, n : n + 1, :] = jnp.broadcast_to(row[None], (out_ref.shape[0], 1, LANES))


def gram(me, xs, rows, copies):
    groups = len(xs)
    count = rows * groups
    return pl.pallas_call(
        functools.partial(gram_kernel, rows, groups),
        out_shape=jax.ShapeDtypeStruct((copies, count * count // LANES, LANES), jnp.float32),
        in_specs=[SMEM_SPEC] + [VMEM_SPEC] * groups,
        out_specs=VMEM_SPEC,
        scratch_shapes=[pltpu.VMEM((count * count, LANES), jnp.float32)],
        compiler_params=pltpu.CompilerParams(vmem_limit_bytes=VMEM_LIMIT),
        cost_estimate=SHORT,
        name="gram",
    )(me, *map(in_vmem, xs))


def add_kernel(*refs):
    refs[-1][...] = sum((ref[...] for ref in refs[1:-1]), refs[0][...])


def add(blocks):
    return pl.pallas_call(
        add_kernel,
        out_shape=jax.ShapeDtypeStruct(blocks[0].shape, blocks[0].dtype),
        in_specs=[VMEM_SPEC] * len(blocks),
        out_specs=VMEM_SPEC,
        compiler_params=pltpu.CompilerParams(vmem_limit_bytes=2**21),
        cost_estimate=SHORT,
        name="add",
    )(*blocks)


def exact(left, right):
    return jnp.dot(left, right, precision=lax.Precision.HIGHEST, preferred_element_type=jnp.float32)


def weights_kernel(rows, count, me_ref, width_ref, *refs):
    grams, drive_ref, repel_ref = refs[:-2], refs[-2], refs[-1]

    def iota(shape, axis):
        return lax.broadcasted_iota(jnp.int32, shape, axis)

    def mask(condition):
        return jnp.where(condition, 1.0, 0.0)

    flat = sum((ref[0] for ref in grams[1:]), grams[0][0])
    lines = flat.shape[0]
    per = LANES // count
    held = exact(mask(iota((count, lines), 0) // per == iota((count, lines), 1)), flat)
    held = jnp.where(iota((count, LANES), 1) // count == iota((count, LANES), 0) % per, held, 0.0)
    inner = exact(held, mask(iota((LANES, count), 0) % count == iota((LANES, count), 1)))
    square = (count, count)
    r, c = iota(square, 0), iota(square, 1)
    order = mask(((me_ref[0] ^ (r // rows)) * rows + r % rows) == c)
    inner = exact(exact(order, inner), order)

    width = width_ref[0]
    diagonal = r == c
    norms = jnp.where(diagonal, inner, 0.0)
    dist = jnp.sum(norms, axis=1, keepdims=True) + jnp.sum(norms, axis=0, keepdims=True) - 2.0 * inner
    kern = jnp.exp(-dist / (width * P_SIZE))
    others = jnp.where(diagonal, 0.0, kern)
    to_drive = kern / count
    to_repel = jnp.where(diagonal, jnp.sum(others, axis=1, keepdims=True), -others) / (count * width)
    for j in range(count):
        drive_ref[j * count : (j + 1) * count, :] = jnp.broadcast_to(to_drive[:, j : j + 1], (count, LANES))
        repel_ref[j * count : (j + 1) * count, :] = jnp.broadcast_to(to_repel[:, j : j + 1], (count, LANES))


def weights(me, width, grams, rows, count):
    shape = jax.ShapeDtypeStruct((count * count, LANES), jnp.float32)
    return pl.pallas_call(
        functools.partial(weights_kernel, rows, count),
        out_shape=(shape, shape),
        in_specs=[SMEM_SPEC, SMEM_SPEC] + [VMEM_SPEC] * len(grams),
        out_specs=(VMEM_SPEC, VMEM_SPEC),
        compiler_params=pltpu.CompilerParams(vmem_limit_bytes=VMEM_LIMIT),
        cost_estimate=SHORT,
        name="weights",
    )(me, width, *grams)


def mix_kernel(rows, count, jobs, drive_ref, repel_ref, *refs):
    blocks = sum(len(spans) for _, _, _, spans in jobs)
    xs, out_ref, scratch = list(refs[:blocks]), refs[blocks], refs[blocks + 1 :]
    streams = [n for n, span in enumerate(span for job in jobs for span in job[3]) if span is not None]
    spans = [span for job in jobs for span in job[3]]
    copies = {}
    for m, n in enumerate(streams):
        start, size = spans[n]
        copies[n] = pltpu.make_async_copy(xs[n].at[pl.ds(start, size), :], scratch[m], scratch[-1].at[m])
        copies[n].start()
        xs[n] = scratch[m]
    step = SUB * rows
    start = used = 0
    for repel, dest, sources, spans in jobs:
        coef_ref = repel_ref if repel else drive_ref
        held = xs[used : used + len(sources)]
        for n in range(used, used + len(sources)):
            if n in copies:
                copies[n].wait()
        used += len(sources)
        steps = held[0].shape[0] // step
        wide = next(w for w in (8, 4, 2, 1) if steps % w == 0)

        def body(t, carry):
            base = pl.multiple_of(t * step * wide, step)
            sums = [[None] * rows for _ in range(wide)]
            for b, source in enumerate(sources):
                for j in range(rows):
                    x = [held[b][pl.ds(base + u * step + j, SUB, stride=rows), :] for u in range(wide)]
                    for i in range(rows):
                        row = (source * rows + j) * count + dest * rows + i
                        c = jnp.broadcast_to(coef_ref[row : row + 1, :], (SUB, LANES))
                        for u in range(wide):
                            term = c * x[u]
                            sums[u][i] = term if sums[u][i] is None else sums[u][i] + term
            for u in range(wide):
                for i in range(rows):
                    out_ref[pl.ds(start + base + u * step + i, SUB, stride=rows), :] = sums[u][i]
            return carry

        lax.fori_loop(0, steps // wide, body, 0)
        start += steps * step


def mix(coefs, rows, count, jobs):
    blocks = [block for job in jobs for block in job[3]]
    streams = [block for block in blocks if isinstance(block, tuple)]
    spans = [(*job[:3], [b[1:] if isinstance(b, tuple) else None for b in job[3]]) for job in jobs]
    size = sum(b[2] if isinstance(b, tuple) else b.shape[0] for b in (job[3][0] for job in jobs))
    scratch = [pltpu.VMEM((block[2], LANES), jnp.float32) for block in streams]
    return pl.pallas_call(
        functools.partial(mix_kernel, rows, count, spans),
        out_shape=jax.ShapeDtypeStruct((size, LANES), jnp.float32),
        in_specs=[VMEM_SPEC] * 2 + [ANY_SPEC if isinstance(block, tuple) else VMEM_SPEC for block in blocks],
        out_specs=VMEM_SPEC,
        scratch_shapes=scratch + ([pltpu.SemaphoreType.DMA((len(streams),))] if streams else []),
        compiler_params=pltpu.CompilerParams(vmem_limit_bytes=VMEM_LIMIT),
        cost_estimate=SHORT,
        name="mix",
    )(*coefs, *[block[0] if isinstance(block, tuple) else in_vmem(block) for block in blocks])


def put_kernel(entries, blocks, me_ref, *refs):
    blocks, (out_ref, sum_ref, sems) = refs[:blocks], refs[-3:]
    copies = []
    used = 0
    for n, (parts, size, place) in enumerate(entries):
        block, start = parts[0]
        source = blocks[block].at[pl.ds(start, size), :]
        if len(parts) > 1:
            total = source[...]
            for block, start in parts[1:]:
                total = total + blocks[block][pl.ds(start, size), :]
            source = sum_ref.at[pl.ds(used, size), :]
            source[...] = total
            used += size
        offset = place[1] if place[0] else (me_ref[0] ^ place[1]) * size
        copy = pltpu.make_async_copy(source, out_ref.at[pl.ds(offset, size), :], sems.at[n])
        copy.start()
        copies.append(copy)
    for copy in copies:
        copy.wait()


def put(me, entries, blocks, size, base=None):
    extra = [] if base is None else [base]
    moved = sum(entry[1] for entry in entries)
    scratch = sum(entry[1] for entry in entries if len(entry[0]) > 1)
    return pl.pallas_call(
        functools.partial(put_kernel, entries, len(blocks)),
        out_shape=jax.ShapeDtypeStruct((size, LANES), jnp.float32),
        in_specs=[SMEM_SPEC] + [VMEM_SPEC] * len(blocks) + [HBM_SPEC] * len(extra),
        out_specs=HBM_SPEC,
        scratch_shapes=[pltpu.VMEM((max(scratch, SUB), LANES), jnp.float32), pltpu.SemaphoreType.DMA((len(entries),))],
        input_output_aliases={1 + len(blocks): 0} if extra else {},
        compiler_params=pltpu.CompilerParams(vmem_limit_bytes=VMEM_LIMIT),
        cost_estimate=pl.CostEstimate(flops=0, bytes_accessed=8 * LANES * moved, transcendentals=0),
        name="put",
    )(me, *blocks, *extra)


def cut_kernel(places, sizes, me_ref, block_ref, *refs):
    outs, (in_sems, out_sems) = refs[: len(sizes)], refs[-2:]
    through = refs[len(sizes) : -2]
    copies = []
    start = 0
    for n, size in enumerate(sizes):
        offset = (me_ref[0] ^ places[n]) * size if places else start
        held = through[n] if through else outs[n]
        copies.append(pltpu.make_async_copy(block_ref.at[pl.ds(offset, size), :], held, in_sems.at[n]))
        copies[n].start()
        start += size
    for copy in copies:
        copy.wait()
    moves = [pltpu.make_async_copy(held, out, out_sems.at[n]) for n, (held, out) in enumerate(zip(through, outs))]
    for move in moves:
        move.start()
    for move in moves:
        move.wait()


def cut(me, block, sizes, places=None):
    out = pltpu.VMEM if places else pltpu.HBM
    through = [] if places else [pltpu.VMEM((size, LANES), jnp.float32) for size in sizes]
    return pl.pallas_call(
        functools.partial(cut_kernel, places, sizes),
        out_shape=[out((size, LANES), jnp.float32) for size in sizes],
        in_specs=[SMEM_SPEC, HBM_SPEC],
        out_specs=[VMEM_SPEC if places else HBM_SPEC] * len(sizes),
        scratch_shapes=through + [pltpu.SemaphoreType.DMA((len(sizes),))] * 2,
        compiler_params=pltpu.CompilerParams(vmem_limit_bytes=VMEM_LIMIT),
        cost_estimate=SHORT,
        name="cut",
    )(me, in_hbm(block))


def shards(particles, scores, kernel_width):
    groups = lax.axis_size("grp")
    rows = particles.shape[0]
    count = rows * groups
    me = lax.axis_index("grp")
    place = me.astype(jnp.int32).reshape(1)
    x, s = dense(particles), dense(scores)
    part, half = x.shape[0] // groups, x.shape[0] // 2
    near = 2 ** ((groups.bit_length() - 1) // 2)
    lows, highs = list(range(near)), list(range(0, groups, near))

    def swap(block, k, axis="grp"):
        return lax.ppermute(block, axis, [(i, i ^ k) for i in range(lax.axis_size(axis))]) if k else block

    def stages(axis):
        left, step = lax.axis_size(axis), 1
        while left > 1:
            radix = 4 if left % 4 == 0 else 2
            yield [step * k for k in range(radix)]
            left, step = left // radix, step * radix

    everyone, others = list(range(groups)), list(range(groups - 1, 0, -1))
    size, step = x.shape[0], SUB * rows
    first = max(1, half // step * 3 // 8) * step
    second = half - first

    sent = cut(place, x, [part] * groups, others + [0])
    s, sent = lax.optimization_barrier((s, sent))
    s_own = cut(place, s, [first, second] * 2)
    xs = {k: swap(block, k) for k, block in zip(others + [0], sent)}
    xs = [xs[k] for k in everyone]

    def exchange(low, high):
        return [swap(low, k) for k in lows], [swap(high, k) for k in highs]

    xs[-1], s_own = lax.optimization_barrier((xs[-1], s_own))
    early = exchange(s_own[0], s_own[2])
    grams = [gram(place, xs, rows, 1)]
    for partners in stages("grp"):
        grams = [swap(add(grams) if len(grams) > 1 else grams[0], k) for k in partners]
    early, pair, grams = lax.optimization_barrier((early, (s_own[1], s_own[3]), grams))
    late = exchange(*pair)
    for partners in stages("par"):
        grams = [swap(add(grams), k, "par") for k in partners]
    coefs = weights(place, kernel_width, grams, rows, count)

    def send(dest, jobs, coefs):
        mixed = mix(coefs, rows, count, jobs)
        return swap(mixed, dest), lax.optimization_barrier((coefs, mixed))[0]

    def score_job(dest, n, held, start, size):
        own = (in_hbm(s), n * half + start, size)
        return (False, dest, (lows, highs)[n], [own] + [(block, 0, size) for block in held[n][1:]])

    near_by = [k for k in others if k in lows or k in highs]
    back, sums = {}, {}
    for k in near_by + [k for k in others if k not in near_by]:
        back[k], coefs = send(k, [(True, k, everyone, xs)], coefs)
    pieces = ((late, first, second), (early, 0, first))
    for p, piece in enumerate(pieces):
        for n, dests in enumerate((highs[1:], lows[1:])):
            for k in dests:
                sums[p, k], coefs = send(k, [score_job(k, n, *piece)], coefs)
    own = mix(coefs, rows, count, [(True, 0, everyone, xs)] + [score_job(0, n, *piece) for piece in pieces for n in (0, 1)])

    repel = put(place, [([(0, 0)], part, (False, 0))], [own], size)
    for k in back:
        repel, back[k] = lax.optimization_barrier((repel, back[k]))
        repel = put(place, [([(0, 0)], part, (False, k))], [back[k]], size, base=repel)
    drive = None
    begin = part
    for p, (held, row, length) in enumerate(pieces):
        entries, blocks = [], [own]
        for n, dests in enumerate((highs[1:], lows[1:])):
            entries.append(([(0, begin)] + [(len(blocks) + m, 0) for m in range(len(dests))], length, (True, n * half + row)))
            blocks += [sums[p, k] for k in dests]
            begin += length
        held = repel if drive is None else (drive, repel)
        held, blocks = lax.optimization_barrier((held, blocks))
        drive, repel = (None, held) if drive is None else held
        drive = put(place, entries, blocks, size, base=drive)
    return (undense(drive, rows), undense(repel, rows))


def solution(mesh):
    return jax.shard_map(
        shards,
        mesh=mesh,
        in_specs=(P("grp", "par"), P("grp", "par"), P()),
        out_specs=(P("grp", "par"), P("grp", "par")),
        check_vma=False,
    )
```

```python
import functools

import jax
import jax.numpy as jnp
from jax import lax
from jax.experimental import pallas as pl
from jax.experimental.pallas import tpu as pltpu
from jax.sharding import PartitionSpec as P

P_SIZE = 1048576
LANES = 128
SUB = 8
VMEM_LIMIT = 16 * 2**20

SMEM_SPEC = pl.BlockSpec(memory_space=pltpu.SMEM)
VMEM_SPEC = pl.BlockSpec(memory_space=pltpu.VMEM)
ANY_SPEC = pl.BlockSpec(memory_space=pl.ANY)
HBM_SPEC = pl.BlockSpec(memory_space=pltpu.HBM)
SHORT = pl.CostEstimate(flops=1, bytes_accessed=1, transcendentals=0)


def in_hbm(array):
    return pltpu.with_memory_space_constraint(array, pltpu.HBM)


def in_vmem(array):
    return pltpu.with_memory_space_constraint(array, pltpu.VMEM)


def dense(block):
    rows, columns = block.shape
    return block.reshape(rows, columns // LANES, LANES).transpose(1, 0, 2).reshape(-1, LANES)


def undense(block, rows):
    return block.reshape(-1, rows, LANES).transpose(1, 0, 2).reshape(rows, -1)


def gram_kernel(rows, groups, *refs):
    xs, out_ref, acc_ref = refs[:groups], refs[groups], refs[groups + 1]
    me = lax.axis_index("grp")
    count = rows * groups
    step = SUB * rows
    steps = xs[0].shape[0] // step

    def load(ref, t, i):
        return ref[pl.ds(t * step + i, SUB, stride=rows), :]

    for a in range(groups):
        for b in range(a, groups):
            pairs = [(i, j) for i in range(rows) for j in range(rows) if a != b or i <= j]

            def body(t, sums):
                left = [load(xs[a], t, i) for i in range(rows)]
                right = left if a == b else [load(xs[b], t, j) for j in range(rows)]
                return tuple(s + left[i] * right[j] for s, (i, j) in zip(sums, pairs))

            zero = jnp.zeros((SUB, LANES), jnp.float32)
            sums = lax.fori_loop(0, steps, body, (zero,) * len(pairs), unroll=2)
            for s, (i, j) in zip(sums, pairs):
                row = jnp.sum(s, axis=0, keepdims=True)
                left, right = (me ^ a) * rows + i, (me ^ b) * rows + j
                acc_ref[pl.ds(left * count + right, 1), :] = row
                if a != b or i != j:
                    acc_ref[pl.ds(right * count + left, 1), :] = row
    total = lax.dot_general(
        jnp.ones((SUB, LANES), jnp.float32),
        acc_ref[...],
        (((1,), (1,)), ((), ())),
        precision=lax.Precision.HIGHEST,
        preferred_element_type=jnp.float32,
    )
    for n in range(count * count // LANES):
        row = total[:1, n * LANES : (n + 1) * LANES]
        out_ref[:, n : n + 1, :] = jnp.broadcast_to(row[None], (out_ref.shape[0], 1, LANES))


def gram(xs, rows, copies):
    groups = len(xs)
    count = rows * groups
    return pl.pallas_call(
        functools.partial(gram_kernel, rows, groups),
        out_shape=jax.ShapeDtypeStruct((copies, count * count // LANES, LANES), jnp.float32),
        in_specs=[VMEM_SPEC] * groups,
        out_specs=VMEM_SPEC,
        scratch_shapes=[pltpu.VMEM((count * count, LANES), jnp.float32)],
        compiler_params=pltpu.CompilerParams(vmem_limit_bytes=VMEM_LIMIT),
        cost_estimate=SHORT,
        name="gram",
    )(*map(in_vmem, xs))


def add_kernel(*refs):
    refs[-1][...] = sum((ref[...] for ref in refs[1:-1]), refs[0][...])


def add(blocks):
    return pl.pallas_call(
        add_kernel,
        out_shape=jax.ShapeDtypeStruct(blocks[0].shape, blocks[0].dtype),
        in_specs=[VMEM_SPEC] * len(blocks),
        out_specs=VMEM_SPEC,
        compiler_params=pltpu.CompilerParams(vmem_limit_bytes=2**21),
        cost_estimate=SHORT,
        name="add",
    )(*blocks)


def exact(left, right):
    return jnp.dot(left, right, precision=lax.Precision.HIGHEST, preferred_element_type=jnp.float32)


def weights_kernel(rows, count, width_ref, *refs):
    me = lax.axis_index("grp")
    grams, drive_ref, repel_ref = refs[:-2], refs[-2], refs[-1]

    def iota(shape, axis):
        return lax.broadcasted_iota(jnp.int32, shape, axis)

    def mask(condition):
        return jnp.where(condition, 1.0, 0.0)

    flat = sum((ref[0] for ref in grams[1:]), grams[0][0])
    lines = flat.shape[0]
    per = LANES // count
    held = exact(mask(iota((count, lines), 0) // per == iota((count, lines), 1)), flat)
    held = jnp.where(iota((count, LANES), 1) // count == iota((count, LANES), 0) % per, held, 0.0)
    inner = exact(held, mask(iota((LANES, count), 0) % count == iota((LANES, count), 1)))
    square = (count, count)
    r, c = iota(square, 0), iota(square, 1)
    order = mask(((me ^ (r // rows)) * rows + r % rows) == c)
    inner = exact(exact(order, inner), order)

    width = width_ref[0]
    diagonal = r == c
    norms = jnp.where(diagonal, inner, 0.0)
    dist = jnp.sum(norms, axis=1, keepdims=True) + jnp.sum(norms, axis=0, keepdims=True) - 2.0 * inner
    kern = jnp.exp(-dist / (width * P_SIZE))
    others = jnp.where(diagonal, 0.0, kern)
    to_drive = kern / count
    to_repel = jnp.where(diagonal, jnp.sum(others, axis=1, keepdims=True), -others) / (count * width)
    for j in range(count):
        drive_ref[j * count : (j + 1) * count, :] = jnp.broadcast_to(to_drive[:, j : j + 1], (count, LANES))
        repel_ref[j * count : (j + 1) * count, :] = jnp.broadcast_to(to_repel[:, j : j + 1], (count, LANES))


def weights(width, grams, rows, count):
    shape = jax.ShapeDtypeStruct((count * count, LANES), jnp.float32)
    return pl.pallas_call(
        functools.partial(weights_kernel, rows, count),
        out_shape=(shape, shape),
        in_specs=[SMEM_SPEC] + [VMEM_SPEC] * len(grams),
        out_specs=(VMEM_SPEC, VMEM_SPEC),
        compiler_params=pltpu.CompilerParams(vmem_limit_bytes=VMEM_LIMIT),
        cost_estimate=SHORT,
        name="weights",
    )(width, *grams)


def mix_kernel(rows, count, jobs, drive_ref, repel_ref, *refs):
    blocks = sum(len(spans) for _, _, _, spans in jobs)
    xs, out_ref, scratch = list(refs[:blocks]), refs[blocks], refs[blocks + 1 :]
    streams = [n for n, span in enumerate(span for job in jobs for span in job[3]) if span is not None]
    spans = [span for job in jobs for span in job[3]]
    copies = {}
    for m, n in enumerate(streams):
        start, size = spans[n]
        copies[n] = pltpu.make_async_copy(xs[n].at[pl.ds(start, size), :], scratch[m], scratch[-1].at[m])
        copies[n].start()
        xs[n] = scratch[m]
    step = SUB * rows
    start = used = 0
    for repel, dest, sources, spans in jobs:
        coef_ref = repel_ref if repel else drive_ref
        held = xs[used : used + len(sources)]
        for n in range(used, used + len(sources)):
            if n in copies:
                copies[n].wait()
        used += len(sources)
        steps = held[0].shape[0] // step
        wide = next(w for w in (8, 4, 2, 1) if steps % w == 0)

        def body(t, carry):
            base = pl.multiple_of(t * step * wide, step)
            sums = [[None] * rows for _ in range(wide)]
            for b, source in enumerate(sources):
                for j in range(rows):
                    x = [held[b][pl.ds(base + u * step + j, SUB, stride=rows), :] for u in range(wide)]
                    for i in range(rows):
                        row = (source * rows + j) * count + dest * rows + i
                        c = jnp.broadcast_to(coef_ref[row : row + 1, :], (SUB, LANES))
                        for u in range(wide):
                            term = c * x[u]
                            sums[u][i] = term if sums[u][i] is None else sums[u][i] + term
            for u in range(wide):
                for i in range(rows):
                    out_ref[pl.ds(start + base + u * step + i, SUB, stride=rows), :] = sums[u][i]
            return carry

        lax.fori_loop(0, steps // wide, body, 0)
        start += steps * step


def mix(coefs, rows, count, jobs):
    blocks = [block for job in jobs for block in job[3]]
    streams = [block for block in blocks if isinstance(block, tuple)]
    spans = [(*job[:3], [b[1:] if isinstance(b, tuple) else None for b in job[3]]) for job in jobs]
    size = sum(b[2] if isinstance(b, tuple) else b.shape[0] for b in (job[3][0] for job in jobs))
    scratch = [pltpu.VMEM((block[2], LANES), jnp.float32) for block in streams]
    return pl.pallas_call(
        functools.partial(mix_kernel, rows, count, spans),
        out_shape=jax.ShapeDtypeStruct((size, LANES), jnp.float32),
        in_specs=[VMEM_SPEC] * 2 + [ANY_SPEC if isinstance(block, tuple) else VMEM_SPEC for block in blocks],
        out_specs=VMEM_SPEC,
        scratch_shapes=scratch + ([pltpu.SemaphoreType.DMA((len(streams),))] if streams else []),
        compiler_params=pltpu.CompilerParams(vmem_limit_bytes=VMEM_LIMIT),
        cost_estimate=SHORT,
        name="mix",
    )(*coefs, *[block[0] if isinstance(block, tuple) else in_vmem(block) for block in blocks])


def put_kernel(entries, blocks, *refs):
    me = lax.axis_index("grp")
    blocks, (out_ref, sum_ref, sems) = refs[:blocks], refs[-3:]
    copies = []
    used = 0
    for n, (parts, size, place) in enumerate(entries):
        block, start = parts[0]
        source = blocks[block].at[pl.ds(start, size), :]
        if len(parts) > 1:
            total = source[...]
            for block, start in parts[1:]:
                total = total + blocks[block][pl.ds(start, size), :]
            source = sum_ref.at[pl.ds(used, size), :]
            source[...] = total
            used += size
        offset = place[1] if place[0] else (me ^ place[1]) * size
        copy = pltpu.make_async_copy(source, out_ref.at[pl.ds(offset, size), :], sems.at[n])
        copy.start()
        copies.append(copy)
    for copy in copies:
        copy.wait()


def put(entries, blocks, size, base=None):
    extra = [] if base is None else [base]
    moved = sum(entry[1] for entry in entries)
    scratch = sum(entry[1] for entry in entries if len(entry[0]) > 1)
    return pl.pallas_call(
        functools.partial(put_kernel, entries, len(blocks)),
        out_shape=jax.ShapeDtypeStruct((size, LANES), jnp.float32),
        in_specs=[VMEM_SPEC] * len(blocks) + [HBM_SPEC] * len(extra),
        out_specs=HBM_SPEC,
        scratch_shapes=[pltpu.VMEM((max(scratch, SUB), LANES), jnp.float32), pltpu.SemaphoreType.DMA((len(entries),))],
        input_output_aliases={len(blocks): 0} if extra else {},
        compiler_params=pltpu.CompilerParams(vmem_limit_bytes=VMEM_LIMIT),
        cost_estimate=pl.CostEstimate(flops=0, bytes_accessed=8 * LANES * moved, transcendentals=0),
        name="put",
    )(*blocks, *extra)


def cut_kernel(places, sizes, block_ref, *refs):
    me = lax.axis_index("grp")
    outs, (in_sems, out_sems) = refs[: len(sizes)], refs[-2:]
    through = refs[len(sizes) : -2]
    copies = []
    start = 0
    for n, size in enumerate(sizes):
        offset = (me ^ places[n]) * size if places else start
        held = through[n] if through else outs[n]
        copies.append(pltpu.make_async_copy(block_ref.at[pl.ds(offset, size), :], held, in_sems.at[n]))
        copies[n].start()
        start += size
    for copy in copies:
        copy.wait()
    moves = [pltpu.make_async_copy(held, out, out_sems.at[n]) for n, (held, out) in enumerate(zip(through, outs))]
    for move in moves:
        move.start()
    for move in moves:
        move.wait()


def cut(block, sizes, places=None):
    out = pltpu.VMEM if places else pltpu.HBM
    through = [] if places else [pltpu.VMEM((size, LANES), jnp.float32) for size in sizes]
    return pl.pallas_call(
        functools.partial(cut_kernel, places, sizes),
        out_shape=[out((size, LANES), jnp.float32) for size in sizes],
        in_specs=[HBM_SPEC],
        out_specs=[VMEM_SPEC if places else HBM_SPEC] * len(sizes),
        scratch_shapes=through + [pltpu.SemaphoreType.DMA((len(sizes),))] * 2,
        compiler_params=pltpu.CompilerParams(vmem_limit_bytes=VMEM_LIMIT),
        cost_estimate=SHORT,
        name="cut",
    )(in_hbm(block))


def shards(particles, scores, kernel_width):
    groups = lax.axis_size("grp")
    rows = particles.shape[0]
    count = rows * groups
    x, s = dense(particles), dense(scores)
    part, half = x.shape[0] // groups, x.shape[0] // 2
    near = 2 ** ((groups.bit_length() - 1) // 2)
    lows, highs = list(range(near)), list(range(0, groups, near))

    def swap(block, k, axis="grp"):
        return lax.ppermute(block, axis, [(i, i ^ k) for i in range(lax.axis_size(axis))]) if k else block

    def stages(axis):
        left, step = lax.axis_size(axis), 1
        while left > 1:
            radix = 4 if left % 4 == 0 else 2
            yield [step * k for k in range(radix)]
            left, step = left // radix, step * radix

    everyone, others = list(range(groups)), list(range(groups - 1, 0, -1))
    size, step = x.shape[0], SUB * rows
    first = max(1, half // step * 3 // 8) * step
    second = half - first

    sent = cut(x, [part] * len(others), others)
    s, sent = lax.optimization_barrier((s, sent))
    s_own = cut(s, [first, second] * 2)
    xs = {k: swap(block, k) for k, block in zip(others, sent)}
    xs[others[0]], x = lax.optimization_barrier((xs[others[0]], x))
    xs[0] = cut(x, [part], [0])[0]
    xs = [xs[k] for k in everyone]

    def exchange(low, high):
        return [swap(low, k) for k in lows], [swap(high, k) for k in highs]

    xs[-1], s_own = lax.optimization_barrier((xs[-1], s_own))
    early = exchange(s_own[0], s_own[2])
    grams = [gram(xs, rows, 1)]
    for partners in stages("grp"):
        grams = [swap(add(grams) if len(grams) > 1 else grams[0], k) for k in partners]
    early, pair, grams = lax.optimization_barrier((early, (s_own[1], s_own[3]), grams))
    late = exchange(*pair)
    for partners in stages("par"):
        grams = [swap(add(grams), k, "par") for k in partners]
    coefs = weights(kernel_width, grams, rows, count)

    s = in_hbm(s)

    def send(dest, jobs, coefs):
        mixed = mix(coefs, rows, count, jobs)
        return swap(mixed, dest), lax.optimization_barrier((coefs, mixed))[0]

    def score_jobs(dest, n, low, high):
        jobs = []
        for held, start, end in ((early, 0, first), (late, first, half)):
            begin, size = max(low, start), min(high, end) - max(low, start)
            if size > 0:
                blocks = [(s, n * half + begin, size)] + [(block, begin - start, size) for block in held[n][1:]]
                jobs.append((False, dest, (lows, highs)[n], blocks))
        return jobs

    back, sums = {}, {}
    for k in others:
        back[k], coefs = send(k, [(True, k, everyone, xs)], coefs)
    middle = half // step // 2 * step
    spans = [span for span in ((0, middle), (middle, half)) if span[0] < span[1]]
    for span in spans:
        for n, dests in enumerate((highs[1:], lows[1:])):
            for k in dests:
                sums[span, k], coefs = send(k, score_jobs(k, n, *span), coefs)
    own_jobs = [(True, 0, everyone, xs)]
    for span in spans:
        own_jobs += score_jobs(0, 0, *span) + score_jobs(0, 1, *span)
    own = mix(coefs, rows, count, own_jobs)

    repel = put([([(0, 0)], part, (False, 0))], [own], size)
    for k in others:
        repel, back[k] = lax.optimization_barrier((repel, back[k]))
        repel = put([([(0, 0)], part, (False, k))], [back[k]], size, base=repel)
    drive = None
    begin = part
    for span in spans:
        length = span[1] - span[0]
        for n, dests in enumerate((highs[1:], lows[1:])):
            got = [sums[span, k] for k in dests]
            held = repel if drive is None else (drive, repel)
            held, got = lax.optimization_barrier((held, got))
            drive, repel = (None, held) if drive is None else held
            entry = ([(0, begin)] + [(1 + m, 0) for m in range(len(got))], length, (True, n * half + span[0]))
            drive = put([entry], [own, *got], size, base=drive)
            begin += length
    return (undense(drive, rows), undense(repel, rows))


def solution(mesh):
    return jax.shard_map(
        shards,
        mesh=mesh,
        in_specs=(P("grp", "par"), P("grp", "par"), P()),
        out_specs=(P("grp", "par"), P("grp", "par")),
        check_vma=False,
    )
```

```python
import functools

import jax
import jax.numpy as jnp
from jax import lax
from jax.experimental import pallas as pl
from jax.experimental.pallas import tpu as pltpu
from jax.sharding import PartitionSpec as P

P_SIZE = 1048576
LANES = 128
SUB = 8
VMEM_LIMIT = 16 * 2**20

SMEM_SPEC = pl.BlockSpec(memory_space=pltpu.SMEM)
VMEM_SPEC = pl.BlockSpec(memory_space=pltpu.VMEM)
ANY_SPEC = pl.BlockSpec(memory_space=pl.ANY)
HBM_SPEC = pl.BlockSpec(memory_space=pltpu.HBM)
SHORT = pl.CostEstimate(flops=1, bytes_accessed=1, transcendentals=0)


def in_hbm(array):
    return pltpu.with_memory_space_constraint(array, pltpu.HBM)


def in_vmem(array):
    return pltpu.with_memory_space_constraint(array, pltpu.VMEM)


def dense(block):
    rows, columns = block.shape
    return block.reshape(rows, columns // LANES, LANES).transpose(1, 0, 2).reshape(-1, LANES)


def undense(block, rows):
    return block.reshape(-1, rows, LANES).transpose(1, 0, 2).reshape(rows, -1)


def gram_kernel(rows, pieces, *refs):
    out_ref, acc_ref = refs[-2], refs[-1]
    me = lax.axis_index("grp")
    groups, count = len(pieces), rows * len(pieces)
    step = SUB * rows
    xs = [refs[sum(pieces[:k]) : sum(pieces[: k + 1])] for k in range(groups)]
    cuts = max(pieces)
    steps = sum(x.shape[0] for x in xs[0]) // step // cuts

    def load(x, cut, t, i):
        ref, base = (x[cut], 0) if len(x) > 1 else (x[0], cut * steps * step)
        return ref[pl.ds(base + t * step + i, SUB, stride=rows), :]

    for a in range(groups):
        for b in range(a, groups):
            pairs = [(i, j) for i in range(rows) for j in range(rows) if a != b or i <= j]
            sums = (jnp.zeros((SUB, LANES), jnp.float32),) * len(pairs)
            for cut in range(cuts):

                def body(t, sums):
                    left = [load(xs[a], cut, t, i) for i in range(rows)]
                    right = left if a == b else [load(xs[b], cut, t, j) for j in range(rows)]
                    return tuple(s + left[i] * right[j] for s, (i, j) in zip(sums, pairs))

                sums = lax.fori_loop(0, steps, body, sums, unroll=2)
            for s, (i, j) in zip(sums, pairs):
                row = jnp.sum(s, axis=0, keepdims=True)
                left, right = (me ^ a) * rows + i, (me ^ b) * rows + j
                acc_ref[pl.ds(left * count + right, 1), :] = row
                if a != b or i != j:
                    acc_ref[pl.ds(right * count + left, 1), :] = row
    total = lax.dot_general(
        jnp.ones((SUB, LANES), jnp.float32),
        acc_ref[...],
        (((1,), (1,)), ((), ())),
        precision=lax.Precision.HIGHEST,
        preferred_element_type=jnp.float32,
    )
    for n in range(count * count // LANES):
        row = total[:1, n * LANES : (n + 1) * LANES]
        out_ref[:, n : n + 1, :] = row[None]


def gram(xs, rows):
    blocks = [block for x in xs for block in x]
    count = rows * len(xs)
    return pl.pallas_call(
        functools.partial(gram_kernel, rows, [len(x) for x in xs]),
        out_shape=jax.ShapeDtypeStruct((1, count * count // LANES, LANES), jnp.float32),
        in_specs=[VMEM_SPEC] * len(blocks),
        out_specs=VMEM_SPEC,
        scratch_shapes=[pltpu.VMEM((count * count, LANES), jnp.float32)],
        compiler_params=pltpu.CompilerParams(vmem_limit_bytes=VMEM_LIMIT),
        cost_estimate=SHORT,
        name="gram",
    )(*map(in_vmem, blocks))


def add_kernel(*refs):
    refs[-1][...] = sum((ref[...] for ref in refs[1:-1]), refs[0][...])


def add(blocks):
    return pl.pallas_call(
        add_kernel,
        out_shape=jax.ShapeDtypeStruct(blocks[0].shape, blocks[0].dtype),
        in_specs=[VMEM_SPEC] * len(blocks),
        out_specs=VMEM_SPEC,
        compiler_params=pltpu.CompilerParams(vmem_limit_bytes=2**21),
        cost_estimate=SHORT,
        name="add",
    )(*blocks)


def exact(left, right):
    return jnp.dot(left, right, precision=lax.Precision.HIGHEST, preferred_element_type=jnp.float32)


def weights_kernel(rows, count, width_ref, *refs):
    me = lax.axis_index("grp")
    grams, drive_ref, repel_ref = refs[:-2], refs[-2], refs[-1]

    def iota(shape, axis):
        return lax.broadcasted_iota(jnp.int32, shape, axis)

    def mask(condition):
        return jnp.where(condition, 1.0, 0.0)

    flat = sum((ref[0] for ref in grams[1:]), grams[0][0])
    lines = flat.shape[0]
    per = LANES // count
    held = exact(mask(iota((count, lines), 0) // per == iota((count, lines), 1)), flat)
    held = jnp.where(iota((count, LANES), 1) // count == iota((count, LANES), 0) % per, held, 0.0)
    inner = exact(held, mask(iota((LANES, count), 0) % count == iota((LANES, count), 1)))
    square = (count, count)
    r, c = iota(square, 0), iota(square, 1)
    order = mask(((me ^ (r // rows)) * rows + r % rows) == c)
    inner = exact(exact(order, inner), order)

    width = width_ref[0]
    diagonal = r == c
    norms = jnp.where(diagonal, inner, 0.0)
    dist = jnp.sum(norms, axis=1, keepdims=True) + jnp.sum(norms, axis=0, keepdims=True) - 2.0 * inner
    kern = jnp.exp(-dist / (width * P_SIZE))
    others = jnp.where(diagonal, 0.0, kern)
    to_drive = kern / count
    to_repel = jnp.where(diagonal, jnp.sum(others, axis=1, keepdims=True), -others) / (count * width)
    for j in range(count):
        drive_ref[j * count : (j + 1) * count, :] = jnp.broadcast_to(to_drive[:, j : j + 1], (count, LANES))
        repel_ref[j * count : (j + 1) * count, :] = jnp.broadcast_to(to_repel[:, j : j + 1], (count, LANES))


def weights(width, grams, rows, count):
    shape = jax.ShapeDtypeStruct((count * count, LANES), jnp.float32)
    return pl.pallas_call(
        functools.partial(weights_kernel, rows, count),
        out_shape=(shape, shape),
        in_specs=[SMEM_SPEC] + [VMEM_SPEC] * len(grams),
        out_specs=(VMEM_SPEC, VMEM_SPEC),
        compiler_params=pltpu.CompilerParams(vmem_limit_bytes=VMEM_LIMIT),
        cost_estimate=SHORT,
        name="weights",
    )(width, *grams)


def mix_kernel(rows, count, jobs, drive_ref, repel_ref, *refs):
    spans = [span for job in jobs for span in job[3]]
    xs, out_ref, scratch = list(refs[: len(spans)]), refs[len(spans)], refs[len(spans) + 1 :]
    offsets = [start for start, _, _ in spans]
    copies = {}
    for n, (start, size, stream) in enumerate(spans):
        if stream:
            m = len(copies)
            copies[n] = pltpu.make_async_copy(xs[n].at[pl.ds(start, size), :], scratch[m], scratch[-1].at[m])
            copies[n].start()
            xs[n], offsets[n] = scratch[m], 0
    step = SUB * rows
    done = used = 0
    for repel, dest, sources, spans in jobs:
        coef_ref = repel_ref if repel else drive_ref
        held = [(xs[n], offsets[n]) for n in range(used, used + len(sources))]
        for n in range(used, used + len(sources)):
            if n in copies:
                copies[n].wait()
        used += len(sources)
        steps = spans[0][1] // step
        wide = next(w for w in (8, 4, 2, 1) if steps % w == 0)

        def body(t, carry):
            base = pl.multiple_of(t * step * wide, step)
            sums = [[None] * rows for _ in range(wide)]
            for (ref, offset), source in zip(held, sources):
                for j in range(rows):
                    x = [ref[pl.ds(offset + base + u * step + j, SUB, stride=rows), :] for u in range(wide)]
                    for i in range(rows):
                        row = (source * rows + j) * count + dest * rows + i
                        c = jnp.broadcast_to(coef_ref[row : row + 1, :], (SUB, LANES))
                        for u in range(wide):
                            term = c * x[u]
                            sums[u][i] = term if sums[u][i] is None else sums[u][i] + term
            for u in range(wide):
                for i in range(rows):
                    out_ref[pl.ds(done + base + u * step + i, SUB, stride=rows), :] = sums[u][i]
            return carry

        lax.fori_loop(0, steps // wide, body, 0)
        done += steps * step


def mix(coefs, rows, count, jobs):
    blocks = [block for job in jobs for block in job[3]]
    streams = [block for block in blocks if block[3]]
    return pl.pallas_call(
        functools.partial(mix_kernel, rows, count, [(*job[:3], [block[1:] for block in job[3]]) for job in jobs]),
        out_shape=jax.ShapeDtypeStruct((sum(job[3][0][2] for job in jobs), LANES), jnp.float32),
        in_specs=[VMEM_SPEC] * 2 + [ANY_SPEC if block[3] else VMEM_SPEC for block in blocks],
        out_specs=VMEM_SPEC,
        scratch_shapes=[pltpu.VMEM((block[2], LANES), jnp.float32) for block in streams]
        + ([pltpu.SemaphoreType.DMA((len(streams),))] if streams else []),
        compiler_params=pltpu.CompilerParams(vmem_limit_bytes=VMEM_LIMIT),
        cost_estimate=SHORT,
        name="mix",
    )(*coefs, *[block[0] if block[3] else in_vmem(block[0]) for block in blocks])


def put_kernel(entries, part, blocks, *refs):
    me = lax.axis_index("grp")
    blocks, (out_ref, sum_ref, sems) = refs[:blocks], refs[-3:]
    copies = []
    used = 0
    for n, (parts, size, (k, row)) in enumerate(entries):
        block, start = parts[0]
        source = blocks[block].at[pl.ds(start, size), :]
        if len(parts) > 1:
            total = source[...]
            for block, start in parts[1:]:
                total = total + blocks[block][pl.ds(start, size), :]
            source = sum_ref.at[pl.ds(used, size), :]
            source[...] = total
            used += size
        offset = row if k is None else (me ^ k) * part + row
        copy = pltpu.make_async_copy(source, out_ref.at[pl.ds(offset, size), :], sems.at[n])
        copy.start()
        copies.append(copy)
    for copy in copies:
        copy.wait()


def put(entries, blocks, part, size, base=None):
    extra = [] if base is None else [base]
    moved = sum(entry[1] for entry in entries)
    scratch = sum(entry[1] for entry in entries if len(entry[0]) > 1)
    return pl.pallas_call(
        functools.partial(put_kernel, entries, part, len(blocks)),
        out_shape=jax.ShapeDtypeStruct((size, LANES), jnp.float32),
        in_specs=[VMEM_SPEC] * len(blocks) + [HBM_SPEC] * len(extra),
        out_specs=HBM_SPEC,
        scratch_shapes=[pltpu.VMEM((max(scratch, SUB), LANES), jnp.float32), pltpu.SemaphoreType.DMA((len(entries),))],
        input_output_aliases={len(blocks): 0} if extra else {},
        compiler_params=pltpu.CompilerParams(vmem_limit_bytes=VMEM_LIMIT),
        cost_estimate=pl.CostEstimate(flops=0, bytes_accessed=8 * LANES * moved, transcendentals=0),
        name="put",
    )(*blocks, *extra)


def cut_kernel(places, part, block_ref, *refs):
    me = lax.axis_index("grp")
    outs, (in_sems, out_sems) = refs[: len(places)], refs[-2:]
    through = refs[len(places) : -2]
    copies = []
    for n, (k, row, size) in enumerate(places):
        offset = row if k is None else (me ^ k) * part + row
        held = through[n] if through else outs[n]
        copies.append(pltpu.make_async_copy(block_ref.at[pl.ds(offset, size), :], held, in_sems.at[n]))
        copies[n].start()
    for copy in copies:
        copy.wait()
    moves = [pltpu.make_async_copy(held, out, out_sems.at[n]) for n, (held, out) in enumerate(zip(through, outs))]
    for move in moves:
        move.start()
    for move in moves:
        move.wait()


def cut(block, places, part, fast):
    out = pltpu.VMEM if fast else pltpu.HBM
    through = [] if fast else [pltpu.VMEM((size, LANES), jnp.float32) for _, _, size in places]
    return pl.pallas_call(
        functools.partial(cut_kernel, places, part),
        out_shape=[out((size, LANES), jnp.float32) for _, _, size in places],
        in_specs=[HBM_SPEC],
        out_specs=[VMEM_SPEC if fast else HBM_SPEC] * len(places),
        scratch_shapes=through + [pltpu.SemaphoreType.DMA((len(places),))] * 2,
        compiler_params=pltpu.CompilerParams(vmem_limit_bytes=VMEM_LIMIT),
        cost_estimate=SHORT,
        name="cut",
    )(in_hbm(block))


def shards(particles, scores, kernel_width):
    groups = lax.axis_size("grp")
    rows = particles.shape[0]
    count = rows * groups
    x, s = dense(particles), dense(scores)
    part, half = x.shape[0] // groups, x.shape[0] // 2
    near = 2 ** ((groups.bit_length() - 1) // 2)
    lows, highs = list(range(near)), list(range(0, groups, near))

    def swap(block, k, axis="grp"):
        return lax.ppermute(block, axis, [(i, i ^ k) for i in range(lax.axis_size(axis))]) if k else block

    def stages(axis):
        left, step = lax.axis_size(axis), 1
        while left > 1:
            radix = 4 if left % 4 == 0 else 2
            yield [step * k for k in range(radix)]
            left, step = left // radix, step * radix

    everyone = list(range(groups))
    direct = [k for k in everyone[1:] if k in lows or k in highs]
    distant = [k for k in everyone[1:] if k not in direct]
    size, step = x.shape[0], SUB * rows
    first = max(1, half // step * 3 // 8) * step
    split = part // step // 2 * step
    halves = [(0, split), (split, part - split)]

    def legs(k, n):
        low, high = k % near, k - k % near
        return (low, high) if n == 0 else (high, low)

    def pieces(k):
        return halves if k in distant else [(0, part)]

    order = distant + direct
    sent = cut(x, [(k, 0, part) for k in order], part, True)
    s, sent = lax.optimization_barrier((s, sent))
    bounds = [(n * half + row, length) for n in (0, 1) for row, length in ((0, first), (first, half - first))]
    s_own = cut(s, [(None, *bound) for bound in bounds], part, False)
    xs = {k: swap(block, k) for k, block in zip(order, sent)}
    xs[order[0]], x, s_own = lax.optimization_barrier((xs[order[0]], x, s_own))
    xs[0] = cut(x, [(0, 0, part)], part, True)[0]
    xs = [[xs[k]] for k in everyone]

    def exchange(low, high):
        return [swap(low, k) for k in lows], [swap(high, k) for k in highs]

    early = exchange(s_own[0], s_own[2])
    grams = [gram(xs, rows)]
    for partners in stages("grp"):
        grams = [swap(add(grams) if len(grams) > 1 else grams[0], k) for k in partners]
    early, pair, grams = lax.optimization_barrier((early, (s_own[1], s_own[3]), grams))
    late = exchange(*pair)
    for partners in stages("par"):
        grams = [swap(add(grams), k, "par") for k in partners]
    coefs = weights(kernel_width, grams, rows, count)

    s = in_hbm(s)

    def send(dest, jobs, coefs):
        mixed = mix(coefs, rows, count, jobs)
        return swap(mixed, dest), lax.optimization_barrier((coefs, mixed))[0]

    def particle_jobs(dest, start, length):
        jobs = []
        for n, (row, piece) in enumerate(halves):
            begin, extent = max(start, row), min(start + length, row + piece) - max(start, row)
            if extent > 0:
                blocks = [(xs[k][n], begin - row, extent, False) if len(xs[k]) > 1 else (xs[k][0], begin, extent, False) for k in everyone]
                jobs.append((True, dest, everyone, blocks))
        return jobs

    def score_jobs(dest, n, low, high):
        jobs = []
        for held, start, end in ((early, 0, first), (late, first, half)):
            begin, extent = max(low, start), min(high, end) - max(low, start)
            if extent > 0:
                blocks = [(s, n * half + begin, extent, True)] + [(block, begin - start, extent, True) for block in held[n][1:]]
                jobs.append((False, dest, (lows, highs)[n], blocks))
        return jobs

    back, sums = {}, {}
    for k in direct:
        back[k, 0], coefs = send(k, particle_jobs(k, 0, part), coefs)
    for k in distant:
        for n in (0, 1):
            hop, coefs = send(legs(k, n)[0], particle_jobs(k, *halves[n]), coefs)
            back[k, n] = swap(hop, legs(k, n)[1])
    middle = half // step // 2 * step
    spans = [span for span in ((0, middle), (middle, half)) if span[0] < span[1]]
    for span in spans:
        for n, dests in enumerate((highs[1:], lows[1:])):
            for k in dests:
                sums[span, k], coefs = send(k, score_jobs(k, n, *span), coefs)
    own_jobs = particle_jobs(0, 0, part)
    for span in spans:
        own_jobs += score_jobs(0, 0, *span) + score_jobs(0, 1, *span)
    own = mix(coefs, rows, count, own_jobs)

    def place(k):
        return [([(n, 0)], length, (k, row)) for n, (row, length) in enumerate(pieces(k))]

    repel = put([([(0, 0)], part, (0, 0))], [own], part, size)
    for k in direct:
        repel, got = lax.optimization_barrier((repel, back[k, 0]))
        repel = put(place(k), [got], part, size, base=repel)
    drive = None
    begin = part
    for span in spans:
        length = span[1] - span[0]
        for n, dests in enumerate((highs[1:], lows[1:])):
            got = [sums[span, k] for k in dests]
            held = repel if drive is None else (drive, repel)
            held, got = lax.optimization_barrier((held, got))
            drive, repel = (None, held) if drive is None else held
            entry = ([(0, begin)] + [(1 + m, 0) for m in range(len(got))], length, (None, n * half + span[0]))
            drive = put([entry], [own, *got], part, size, base=drive)
            begin += length
    for k in distant:
        got = [back[k, n] for n in (0, 1)]
        (drive, repel), got = lax.optimization_barrier(((drive, repel), got))
        repel = put(place(k), got, part, size, base=repel)
    return (undense(drive, rows), undense(repel, rows))


def solution(mesh):
    return jax.shard_map(
        shards,
        mesh=mesh,
        in_specs=(P("grp", "par"), P("grp", "par"), P()),
        out_specs=(P("grp", "par"), P("grp", "par")),
        check_vma=False,
    )
```

```python
import functools

import jax
import jax.numpy as jnp
from jax import lax
from jax.experimental import pallas as pl
from jax.experimental.pallas import tpu as pltpu
from jax.sharding import PartitionSpec as P

P_SIZE = 1048576
LANES = 128
SUB = 8
VMEM_LIMIT = 16 * 2**20

SMEM_SPEC = pl.BlockSpec(memory_space=pltpu.SMEM)
VMEM_SPEC = pl.BlockSpec(memory_space=pltpu.VMEM)
ANY_SPEC = pl.BlockSpec(memory_space=pl.ANY)
HBM_SPEC = pl.BlockSpec(memory_space=pltpu.HBM)
SHORT = pl.CostEstimate(flops=1, bytes_accessed=1, transcendentals=0)


def in_hbm(array):
    return pltpu.with_memory_space_constraint(array, pltpu.HBM)


def in_vmem(array):
    return pltpu.with_memory_space_constraint(array, pltpu.VMEM)


def dense(block):
    rows, columns = block.shape
    return block.reshape(rows, columns // LANES, LANES).transpose(1, 0, 2).reshape(-1, LANES)


def undense(block, rows):
    return block.reshape(-1, rows, LANES).transpose(1, 0, 2).reshape(rows, -1)


def gram_kernel(rows, pieces, *refs):
    out_ref, acc_ref = refs[-2], refs[-1]
    me = lax.axis_index("grp")
    groups, count = len(pieces), rows * len(pieces)
    step = SUB * rows
    xs = [refs[sum(pieces[:k]) : sum(pieces[: k + 1])] for k in range(groups)]
    cuts = max(pieces)
    steps = sum(x.shape[0] for x in xs[0]) // step // cuts

    def load(x, cut, t, i):
        ref, base = (x[cut], 0) if len(x) > 1 else (x[0], cut * steps * step)
        return ref[pl.ds(base + t * step + i, SUB, stride=rows), :]

    for a in range(groups):
        for b in range(a, groups):
            pairs = [(i, j) for i in range(rows) for j in range(rows) if a != b or i <= j]
            sums = (jnp.zeros((SUB, LANES), jnp.float32),) * len(pairs)
            for cut in range(cuts):

                def body(t, sums):
                    left = [load(xs[a], cut, t, i) for i in range(rows)]
                    right = left if a == b else [load(xs[b], cut, t, j) for j in range(rows)]
                    return tuple(s + left[i] * right[j] for s, (i, j) in zip(sums, pairs))

                sums = lax.fori_loop(0, steps, body, sums, unroll=2)
            for s, (i, j) in zip(sums, pairs):
                row = jnp.sum(s, axis=0, keepdims=True)
                left, right = (me ^ a) * rows + i, (me ^ b) * rows + j
                acc_ref[pl.ds(left * count + right, 1), :] = row
                if a != b or i != j:
                    acc_ref[pl.ds(right * count + left, 1), :] = row
    total = lax.dot_general(
        jnp.ones((SUB, LANES), jnp.float32),
        acc_ref[...],
        (((1,), (1,)), ((), ())),
        precision=lax.Precision.HIGHEST,
        preferred_element_type=jnp.float32,
    )
    for n in range(count * count // LANES):
        row = total[:1, n * LANES : (n + 1) * LANES]
        out_ref[:, n : n + 1, :] = row[None]


def gram(xs, rows):
    blocks = [block for x in xs for block in x]
    count = rows * len(xs)
    return pl.pallas_call(
        functools.partial(gram_kernel, rows, [len(x) for x in xs]),
        out_shape=jax.ShapeDtypeStruct((1, count * count // LANES, LANES), jnp.float32),
        in_specs=[VMEM_SPEC] * len(blocks),
        out_specs=VMEM_SPEC,
        scratch_shapes=[pltpu.VMEM((count * count, LANES), jnp.float32)],
        compiler_params=pltpu.CompilerParams(vmem_limit_bytes=VMEM_LIMIT),
        cost_estimate=SHORT,
        name="gram",
    )(*map(in_vmem, blocks))


def add_kernel(*refs):
    refs[-1][...] = sum((ref[...] for ref in refs[1:-1]), refs[0][...])


def add(blocks):
    return pl.pallas_call(
        add_kernel,
        out_shape=jax.ShapeDtypeStruct(blocks[0].shape, blocks[0].dtype),
        in_specs=[VMEM_SPEC] * len(blocks),
        out_specs=VMEM_SPEC,
        compiler_params=pltpu.CompilerParams(vmem_limit_bytes=2**21),
        cost_estimate=SHORT,
        name="add",
    )(*blocks)


def exact(left, right):
    return jnp.dot(left, right, precision=lax.Precision.HIGHEST, preferred_element_type=jnp.float32)


def weights_kernel(rows, count, width_ref, *refs):
    me = lax.axis_index("grp")
    grams, drive_ref, repel_ref = refs[:-2], refs[-2], refs[-1]

    def iota(shape, axis):
        return lax.broadcasted_iota(jnp.int32, shape, axis)

    def mask(condition):
        return jnp.where(condition, 1.0, 0.0)

    flat = sum((ref[0] for ref in grams[1:]), grams[0][0])
    lines = flat.shape[0]
    per = LANES // count
    held = exact(mask(iota((count, lines), 0) // per == iota((count, lines), 1)), flat)
    held = jnp.where(iota((count, LANES), 1) // count == iota((count, LANES), 0) % per, held, 0.0)
    inner = exact(held, mask(iota((LANES, count), 0) % count == iota((LANES, count), 1)))
    square = (count, count)
    r, c = iota(square, 0), iota(square, 1)
    order = mask(((me ^ (r // rows)) * rows + r % rows) == c)
    inner = exact(exact(order, inner), order)

    width = width_ref[0]
    diagonal = r == c
    norms = jnp.where(diagonal, inner, 0.0)
    dist = jnp.sum(norms, axis=1, keepdims=True) + jnp.sum(norms, axis=0, keepdims=True) - 2.0 * inner
    kern = jnp.exp(-dist / (width * P_SIZE))
    others = jnp.where(diagonal, 0.0, kern)
    to_drive = kern / count
    to_repel = jnp.where(diagonal, jnp.sum(others, axis=1, keepdims=True), -others) / (count * width)
    for j in range(count):
        drive_ref[j * count : (j + 1) * count, :] = jnp.broadcast_to(to_drive[:, j : j + 1], (count, LANES))
        repel_ref[j * count : (j + 1) * count, :] = jnp.broadcast_to(to_repel[:, j : j + 1], (count, LANES))


def weights(width, grams, rows, count):
    shape = jax.ShapeDtypeStruct((count * count, LANES), jnp.float32)
    return pl.pallas_call(
        functools.partial(weights_kernel, rows, count),
        out_shape=(shape, shape),
        in_specs=[SMEM_SPEC] + [VMEM_SPEC] * len(grams),
        out_specs=(VMEM_SPEC, VMEM_SPEC),
        compiler_params=pltpu.CompilerParams(vmem_limit_bytes=VMEM_LIMIT),
        cost_estimate=SHORT,
        name="weights",
    )(width, *grams)


def mix_kernel(rows, count, jobs, drive_ref, repel_ref, *refs):
    spans = [span for job in jobs for span in job[3]]
    xs, out_ref, scratch = list(refs[: len(spans)]), refs[len(spans)], refs[len(spans) + 1 :]
    offsets = [start for start, _, _ in spans]
    copies = {}
    for n, (start, size, stream) in enumerate(spans):
        if stream:
            m = len(copies)
            copies[n] = pltpu.make_async_copy(xs[n].at[pl.ds(start, size), :], scratch[m], scratch[-1].at[m])
            copies[n].start()
            xs[n], offsets[n] = scratch[m], 0
    step = SUB * rows
    done = used = 0
    for repel, dest, sources, spans in jobs:
        coef_ref = repel_ref if repel else drive_ref
        held = [(xs[n], offsets[n]) for n in range(used, used + len(sources))]
        for n in range(used, used + len(sources)):
            if n in copies:
                copies[n].wait()
        used += len(sources)
        steps = spans[0][1] // step
        wide = next(w for w in (8, 4, 2, 1) if steps % w == 0)

        def body(t, carry):
            base = pl.multiple_of(t * step * wide, step)
            sums = [[None] * rows for _ in range(wide)]
            for (ref, offset), source in zip(held, sources):
                for j in range(rows):
                    x = [ref[pl.ds(offset + base + u * step + j, SUB, stride=rows), :] for u in range(wide)]
                    for i in range(rows):
                        row = (source * rows + j) * count + dest * rows + i
                        c = jnp.broadcast_to(coef_ref[row : row + 1, :], (SUB, LANES))
                        for u in range(wide):
                            term = c * x[u]
                            sums[u][i] = term if sums[u][i] is None else sums[u][i] + term
            for u in range(wide):
                for i in range(rows):
                    out_ref[pl.ds(done + base + u * step + i, SUB, stride=rows), :] = sums[u][i]
            return carry

        lax.fori_loop(0, steps // wide, body, 0)
        done += steps * step


def mix(coefs, rows, count, jobs):
    blocks = [block for job in jobs for block in job[3]]
    streams = [block for block in blocks if block[3]]
    return pl.pallas_call(
        functools.partial(mix_kernel, rows, count, [(*job[:3], [block[1:] for block in job[3]]) for job in jobs]),
        out_shape=jax.ShapeDtypeStruct((sum(job[3][0][2] for job in jobs), LANES), jnp.float32),
        in_specs=[VMEM_SPEC] * 2 + [ANY_SPEC if block[3] else VMEM_SPEC for block in blocks],
        out_specs=VMEM_SPEC,
        scratch_shapes=[pltpu.VMEM((block[2], LANES), jnp.float32) for block in streams]
        + ([pltpu.SemaphoreType.DMA((len(streams),))] if streams else []),
        compiler_params=pltpu.CompilerParams(vmem_limit_bytes=VMEM_LIMIT),
        cost_estimate=SHORT,
        name="mix",
    )(*coefs, *[block[0] if block[3] else in_vmem(block[0]) for block in blocks])


def put_kernel(entries, part, blocks, *refs):
    me = lax.axis_index("grp")
    blocks, (out_ref, sum_ref, sems) = refs[:blocks], refs[-3:]
    copies = []
    used = 0
    for n, (parts, size, (k, row)) in enumerate(entries):
        block, start = parts[0]
        source = blocks[block].at[pl.ds(start, size), :]
        if len(parts) > 1:
            total = source[...]
            for block, start in parts[1:]:
                total = total + blocks[block][pl.ds(start, size), :]
            source = sum_ref.at[pl.ds(used, size), :]
            source[...] = total
            used += size
        offset = row if k is None else (me ^ k) * part + row
        copy = pltpu.make_async_copy(source, out_ref.at[pl.ds(offset, size), :], sems.at[n])
        copy.start()
        copies.append(copy)
    for copy in copies:
        copy.wait()


def put(entries, blocks, part, size, base=None):
    extra = [] if base is None else [base]
    moved = sum(entry[1] for entry in entries)
    scratch = sum(entry[1] for entry in entries if len(entry[0]) > 1)
    return pl.pallas_call(
        functools.partial(put_kernel, entries, part, len(blocks)),
        out_shape=jax.ShapeDtypeStruct((size, LANES), jnp.float32),
        in_specs=[VMEM_SPEC] * len(blocks) + [HBM_SPEC] * len(extra),
        out_specs=HBM_SPEC,
        scratch_shapes=[pltpu.VMEM((max(scratch, SUB), LANES), jnp.float32), pltpu.SemaphoreType.DMA((len(entries),))],
        input_output_aliases={len(blocks): 0} if extra else {},
        compiler_params=pltpu.CompilerParams(vmem_limit_bytes=VMEM_LIMIT),
        cost_estimate=pl.CostEstimate(flops=0, bytes_accessed=8 * LANES * moved, transcendentals=0),
        name="put",
    )(*blocks, *extra)


def cut_kernel(places, part, block_ref, *refs):
    me = lax.axis_index("grp")
    outs, (in_sems, out_sems) = refs[: len(places)], refs[-2:]
    through = refs[len(places) : -2]
    copies = []
    for n, (k, row, size) in enumerate(places):
        offset = row if k is None else (me ^ k) * part + row
        held = through[n] if through else outs[n]
        copies.append(pltpu.make_async_copy(block_ref.at[pl.ds(offset, size), :], held, in_sems.at[n]))
        copies[n].start()
    for copy in copies:
        copy.wait()
    moves = [pltpu.make_async_copy(held, out, out_sems.at[n]) for n, (held, out) in enumerate(zip(through, outs))]
    for move in moves:
        move.start()
    for move in moves:
        move.wait()


def cut(block, places, part, fast):
    out = pltpu.VMEM if fast else pltpu.HBM
    through = [] if fast else [pltpu.VMEM((size, LANES), jnp.float32) for _, _, size in places]
    return pl.pallas_call(
        functools.partial(cut_kernel, places, part),
        out_shape=[out((size, LANES), jnp.float32) for _, _, size in places],
        in_specs=[HBM_SPEC],
        out_specs=[VMEM_SPEC if fast else HBM_SPEC] * len(places),
        scratch_shapes=through + [pltpu.SemaphoreType.DMA((len(places),))] * 2,
        compiler_params=pltpu.CompilerParams(vmem_limit_bytes=VMEM_LIMIT),
        cost_estimate=SHORT,
        name="cut",
    )(in_hbm(block))


def shards(particles, scores, kernel_width):
    groups = lax.axis_size("grp")
    rows = particles.shape[0]
    count = rows * groups
    x, s = dense(particles), dense(scores)
    part, half = x.shape[0] // groups, x.shape[0] // 2
    near = 2 ** ((groups.bit_length() - 1) // 2)
    lows, highs = list(range(near)), list(range(0, groups, near))

    def swap(block, k, axis="grp"):
        return lax.ppermute(block, axis, [(i, i ^ k) for i in range(lax.axis_size(axis))]) if k else block

    def stages(axis):
        left, step = lax.axis_size(axis), 1
        while left > 1:
            radix = 4 if left % 4 == 0 else 2
            yield [step * k for k in range(radix)]
            left, step = left // radix, step * radix

    everyone = list(range(groups))
    direct = [k for k in everyone[1:] if k in lows or k in highs]
    distant = [k for k in everyone[1:] if k not in direct]
    size, step = x.shape[0], SUB * rows
    first = max(1, half // step * 3 // 8) * step
    split = part // step // 2 * step
    halves = [(0, split), (split, part - split)]

    def legs(k, n):
        low, high = k % near, k - k % near
        return (low, high) if n == 0 else (high, low)

    def pieces(k):
        return halves if k in distant else [(0, part)]

    order = distant + direct
    sent = cut(x, [(k, 0, part) for k in order], part, True)
    s, sent = lax.optimization_barrier((s, sent))
    bounds = [(n * half + row, length) for n in (0, 1) for row, length in ((0, first), (first, half - first))]
    s_own = cut(s, [(None, *bound) for bound in bounds], part, False)
    xs = {k: swap(block, k) for k, block in zip(order, sent)}
    xs[order[0]], x, s_own = lax.optimization_barrier((xs[order[0]], x, s_own))
    xs[0] = cut(x, [(0, 0, part)], part, True)[0]
    xs = [[xs[k]] for k in everyone]

    def exchange(block, partners):
        return [swap(block, k) for k in partners]

    early = [exchange(s_own[0], lows), exchange(s_own[2], highs)]
    grams = [gram(xs, rows)]
    pair = [s_own[1], s_own[3]]
    for partners in stages("grp"):
        total = add(grams) if len(grams) > 1 else grams[0]
        grams = [swap(total, k) for k in partners]
    early, pair, grams = lax.optimization_barrier((early, pair, grams))
    late = [exchange(pair[0], lows), exchange(pair[1], highs)]
    for partners in stages("par"):
        grams = [swap(add(grams), k, "par") for k in partners]
    coefs = weights(kernel_width, grams, rows, count)

    s = in_hbm(s)

    def send(dest, jobs, coefs):
        mixed = mix(coefs, rows, count, jobs)
        return swap(mixed, dest), lax.optimization_barrier((coefs, mixed))[0]

    def particle_jobs(dest, start, length):
        jobs = []
        for n, (row, piece) in enumerate(halves):
            begin, extent = max(start, row), min(start + length, row + piece) - max(start, row)
            if extent > 0:
                blocks = [(xs[k][n], begin - row, extent, False) if len(xs[k]) > 1 else (xs[k][0], begin, extent, False) for k in everyone]
                jobs.append((True, dest, everyone, blocks))
        return jobs

    def score_jobs(dest, n, low, high):
        jobs = []
        for held, start, end in ((early, 0, first), (late, first, half)):
            begin, extent = max(low, start), min(high, end) - max(low, start)
            if extent > 0:
                blocks = [(s, n * half + begin, extent, True)] + [(block, begin - start, extent, True) for block in held[n][1:]]
                jobs.append((False, dest, (lows, highs)[n], blocks))
        return jobs

    back, sums = {}, {}
    for k in direct:
        back[k, 0], coefs = send(k, particle_jobs(k, 0, part), coefs)
    for k in distant:
        for n in (1, 0):
            hop, coefs = send(legs(k, n)[0], particle_jobs(k, *halves[n]), coefs)
            back[k, n] = swap(hop, legs(k, n)[1])
    middle = half // step // 2 * step
    spans = [span for span in ((0, middle), (middle, half)) if span[0] < span[1]]
    for span in spans:
        for n, dests in enumerate((highs[1:], lows[1:])):
            for k in dests:
                sums[span, k], coefs = send(k, score_jobs(k, n, *span), coefs)
    own_jobs = particle_jobs(0, 0, part)
    for span in spans:
        own_jobs += score_jobs(0, 0, *span) + score_jobs(0, 1, *span)
    own = mix(coefs, rows, count, own_jobs)

    def place(k):
        return [([(n, 0)], length, (k, row)) for n, (row, length) in enumerate(pieces(k))]

    repel = put([([(0, 0)], part, (0, 0))], [own], part, size)
    for k in direct:
        repel, got = lax.optimization_barrier((repel, back[k, 0]))
        repel = put(place(k), [got], part, size, base=repel)
    drive = None
    begin = part
    for span in spans:
        length = span[1] - span[0]
        for n, dests in enumerate((highs[1:], lows[1:])):
            got = [sums[span, k] for k in dests]
            held = repel if drive is None else (drive, repel)
            held, got = lax.optimization_barrier((held, got))
            drive, repel = (None, held) if drive is None else held
            entry = ([(0, begin)] + [(1 + m, 0) for m in range(len(got))], length, (None, n * half + span[0]))
            drive = put([entry], [own, *got], part, size, base=drive)
            begin += length
    for k in distant:
        got = [back[k, n] for n in (0, 1)]
        (drive, repel), got = lax.optimization_barrier(((drive, repel), got))
        repel = put(place(k), got, part, size, base=repel)
    return (undense(drive, rows), undense(repel, rows))


def solution(mesh):
    return jax.shard_map(
        shards,
        mesh=mesh,
        in_specs=(P("grp", "par"), P("grp", "par"), P()),
        out_specs=(P("grp", "par"), P("grp", "par")),
        check_vma=False,
    )
```

```python
import functools

import jax
import jax.numpy as jnp
from jax import lax
from jax.experimental import pallas as pl
from jax.experimental.pallas import tpu as pltpu
from jax.sharding import PartitionSpec as P

P_SIZE = 1048576
LANES = 128
SUB = 8
VMEM_LIMIT = 16 * 2**20

SMEM_SPEC = pl.BlockSpec(memory_space=pltpu.SMEM)
VMEM_SPEC = pl.BlockSpec(memory_space=pltpu.VMEM)
ANY_SPEC = pl.BlockSpec(memory_space=pl.ANY)
HBM_SPEC = pl.BlockSpec(memory_space=pltpu.HBM)
SHORT = pl.CostEstimate(flops=1, bytes_accessed=1, transcendentals=0)


def in_hbm(array):
    return pltpu.with_memory_space_constraint(array, pltpu.HBM)


def in_vmem(array):
    return pltpu.with_memory_space_constraint(array, pltpu.VMEM)


def dense(block):
    rows, columns = block.shape
    return block.reshape(rows, columns // LANES, LANES).transpose(1, 0, 2).reshape(-1, LANES)


def undense(block, rows):
    return block.reshape(-1, rows, LANES).transpose(1, 0, 2).reshape(rows, -1)


def gram_kernel(rows, pieces, *refs):
    out_ref, acc_ref = refs[-2], refs[-1]
    me = lax.axis_index("grp")
    groups, count = len(pieces), rows * len(pieces)
    step = SUB * rows
    xs = [refs[sum(pieces[:k]) : sum(pieces[: k + 1])] for k in range(groups)]
    cuts = max(pieces)
    steps = sum(x.shape[0] for x in xs[0]) // step // cuts

    def load(x, cut, t, i):
        ref, base = (x[cut], 0) if len(x) > 1 else (x[0], cut * steps * step)
        return ref[pl.ds(base + t * step + i, SUB, stride=rows), :]

    for a in range(groups):
        for b in range(a, groups):
            pairs = [(i, j) for i in range(rows) for j in range(rows) if a != b or i <= j]
            sums = (jnp.zeros((SUB, LANES), jnp.float32),) * len(pairs)
            for cut in range(cuts):

                def body(t, sums):
                    left = [load(xs[a], cut, t, i) for i in range(rows)]
                    right = left if a == b else [load(xs[b], cut, t, j) for j in range(rows)]
                    return tuple(s + left[i] * right[j] for s, (i, j) in zip(sums, pairs))

                sums = lax.fori_loop(0, steps, body, sums, unroll=2)
            for s, (i, j) in zip(sums, pairs):
                row = jnp.sum(s, axis=0, keepdims=True)
                left, right = (me ^ a) * rows + i, (me ^ b) * rows + j
                acc_ref[pl.ds(left * count + right, 1), :] = row
                if a != b or i != j:
                    acc_ref[pl.ds(right * count + left, 1), :] = row
    total = lax.dot_general(
        jnp.ones((SUB, LANES), jnp.float32),
        acc_ref[...],
        (((1,), (1,)), ((), ())),
        precision=lax.Precision.HIGHEST,
        preferred_element_type=jnp.float32,
    )
    for n in range(count * count // LANES):
        row = total[:1, n * LANES : (n + 1) * LANES]
        out_ref[:, n : n + 1, :] = row[None]


def gram(xs, rows):
    blocks = [block for x in xs for block in x]
    count = rows * len(xs)
    return pl.pallas_call(
        functools.partial(gram_kernel, rows, [len(x) for x in xs]),
        out_shape=jax.ShapeDtypeStruct((1, count * count // LANES, LANES), jnp.float32),
        in_specs=[VMEM_SPEC] * len(blocks),
        out_specs=VMEM_SPEC,
        scratch_shapes=[pltpu.VMEM((count * count, LANES), jnp.float32)],
        compiler_params=pltpu.CompilerParams(vmem_limit_bytes=VMEM_LIMIT),
        cost_estimate=SHORT,
        name="gram",
    )(*map(in_vmem, blocks))


def add_kernel(*refs):
    refs[-1][...] = sum((ref[...] for ref in refs[1:-1]), refs[0][...])


def add(blocks):
    return pl.pallas_call(
        add_kernel,
        out_shape=jax.ShapeDtypeStruct(blocks[0].shape, blocks[0].dtype),
        in_specs=[VMEM_SPEC] * len(blocks),
        out_specs=VMEM_SPEC,
        compiler_params=pltpu.CompilerParams(vmem_limit_bytes=2**21),
        cost_estimate=SHORT,
        name="add",
    )(*blocks)


def exact(left, right):
    return jnp.dot(left, right, precision=lax.Precision.HIGHEST, preferred_element_type=jnp.float32)


def weights_kernel(rows, count, width_ref, *refs):
    me = lax.axis_index("grp")
    grams, drive_ref, repel_ref = refs[:-2], refs[-2], refs[-1]

    def iota(shape, axis):
        return lax.broadcasted_iota(jnp.int32, shape, axis)

    def mask(condition):
        return jnp.where(condition, 1.0, 0.0)

    flat = sum((ref[0] for ref in grams[1:]), grams[0][0])
    lines = flat.shape[0]
    per = LANES // count
    held = exact(mask(iota((count, lines), 0) // per == iota((count, lines), 1)), flat)
    held = jnp.where(iota((count, LANES), 1) // count == iota((count, LANES), 0) % per, held, 0.0)
    inner = exact(held, mask(iota((LANES, count), 0) % count == iota((LANES, count), 1)))
    square = (count, count)
    r, c = iota(square, 0), iota(square, 1)
    order = mask(((me ^ (r // rows)) * rows + r % rows) == c)
    inner = exact(exact(order, inner), order)

    width = width_ref[0]
    diagonal = r == c
    norms = jnp.where(diagonal, inner, 0.0)
    dist = jnp.sum(norms, axis=1, keepdims=True) + jnp.sum(norms, axis=0, keepdims=True) - 2.0 * inner
    kern = jnp.exp(-dist / (width * P_SIZE))
    others = jnp.where(diagonal, 0.0, kern)
    to_drive = kern / count
    to_repel = jnp.where(diagonal, jnp.sum(others, axis=1, keepdims=True), -others) / (count * width)
    for j in range(count):
        drive_ref[j * count : (j + 1) * count, :] = jnp.broadcast_to(to_drive[:, j : j + 1], (count, LANES))
        repel_ref[j * count : (j + 1) * count, :] = jnp.broadcast_to(to_repel[:, j : j + 1], (count, LANES))


def weights(width, grams, rows, count):
    shape = jax.ShapeDtypeStruct((count * count, LANES), jnp.float32)
    return pl.pallas_call(
        functools.partial(weights_kernel, rows, count),
        out_shape=(shape, shape),
        in_specs=[SMEM_SPEC] + [VMEM_SPEC] * len(grams),
        out_specs=(VMEM_SPEC, VMEM_SPEC),
        compiler_params=pltpu.CompilerParams(vmem_limit_bytes=VMEM_LIMIT),
        cost_estimate=SHORT,
        name="weights",
    )(width, *grams)


def mix_kernel(rows, count, jobs, drive_ref, repel_ref, *refs):
    spans = [span for job in jobs for span in job[3]]
    xs, out_ref, scratch = list(refs[: len(spans)]), refs[len(spans)], refs[len(spans) + 1 :]
    offsets = [start for start, _, _ in spans]
    copies = {}
    for n, (start, size, stream) in enumerate(spans):
        if stream:
            m = len(copies)
            copies[n] = pltpu.make_async_copy(xs[n].at[pl.ds(start, size), :], scratch[m], scratch[-1].at[m])
            copies[n].start()
            xs[n], offsets[n] = scratch[m], 0
    step = SUB * rows
    done = used = 0
    for repel, dest, sources, spans in jobs:
        coef_ref = repel_ref if repel else drive_ref
        held = [(xs[n], offsets[n]) for n in range(used, used + len(sources))]
        for n in range(used, used + len(sources)):
            if n in copies:
                copies[n].wait()
        used += len(sources)
        steps = spans[0][1] // step
        wide = next(w for w in (8, 4, 2, 1) if steps % w == 0)

        def body(t, carry):
            base = pl.multiple_of(t * step * wide, step)
            sums = [[None] * rows for _ in range(wide)]
            for (ref, offset), source in zip(held, sources):
                for j in range(rows):
                    x = [ref[pl.ds(offset + base + u * step + j, SUB, stride=rows), :] for u in range(wide)]
                    for i in range(rows):
                        row = (source * rows + j) * count + dest * rows + i
                        c = jnp.broadcast_to(coef_ref[row : row + 1, :], (SUB, LANES))
                        for u in range(wide):
                            term = c * x[u]
                            sums[u][i] = term if sums[u][i] is None else sums[u][i] + term
            for u in range(wide):
                for i in range(rows):
                    out_ref[pl.ds(done + base + u * step + i, SUB, stride=rows), :] = sums[u][i]
            return carry

        lax.fori_loop(0, steps // wide, body, 0)
        done += steps * step


def mix(coefs, rows, count, jobs):
    blocks = [block for job in jobs for block in job[3]]
    streams = [block for block in blocks if block[3]]
    return pl.pallas_call(
        functools.partial(mix_kernel, rows, count, [(*job[:3], [block[1:] for block in job[3]]) for job in jobs]),
        out_shape=jax.ShapeDtypeStruct((sum(job[3][0][2] for job in jobs), LANES), jnp.float32),
        in_specs=[VMEM_SPEC] * 2 + [ANY_SPEC if block[3] else VMEM_SPEC for block in blocks],
        out_specs=VMEM_SPEC,
        scratch_shapes=[pltpu.VMEM((block[2], LANES), jnp.float32) for block in streams]
        + ([pltpu.SemaphoreType.DMA((len(streams),))] if streams else []),
        compiler_params=pltpu.CompilerParams(vmem_limit_bytes=VMEM_LIMIT),
        cost_estimate=SHORT,
        name="mix",
    )(*coefs, *[block[0] if block[3] else in_vmem(block[0]) for block in blocks])


def put_kernel(entries, part, blocks, *refs):
    me = lax.axis_index("grp")
    blocks, (out_ref, sum_ref, sems) = refs[:blocks], refs[-3:]
    copies = []
    used = 0
    for n, (parts, size, (k, row)) in enumerate(entries):
        block, start = parts[0]
        source = blocks[block].at[pl.ds(start, size), :]
        if len(parts) > 1:
            total = source[...]
            for block, start in parts[1:]:
                total = total + blocks[block][pl.ds(start, size), :]
            source = sum_ref.at[pl.ds(used, size), :]
            source[...] = total
            used += size
        offset = row if k is None else (me ^ k) * part + row
        copy = pltpu.make_async_copy(source, out_ref.at[pl.ds(offset, size), :], sems.at[n])
        copy.start()
        copies.append(copy)
    for copy in copies:
        copy.wait()


def put(entries, blocks, part, size, base=None):
    extra = [] if base is None else [base]
    moved = sum(entry[1] for entry in entries)
    scratch = sum(entry[1] for entry in entries if len(entry[0]) > 1)
    return pl.pallas_call(
        functools.partial(put_kernel, entries, part, len(blocks)),
        out_shape=jax.ShapeDtypeStruct((size, LANES), jnp.float32),
        in_specs=[VMEM_SPEC] * len(blocks) + [HBM_SPEC] * len(extra),
        out_specs=HBM_SPEC,
        scratch_shapes=[pltpu.VMEM((max(scratch, SUB), LANES), jnp.float32), pltpu.SemaphoreType.DMA((len(entries),))],
        input_output_aliases={len(blocks): 0} if extra else {},
        compiler_params=pltpu.CompilerParams(vmem_limit_bytes=VMEM_LIMIT),
        cost_estimate=pl.CostEstimate(flops=0, bytes_accessed=8 * LANES * moved, transcendentals=0),
        name="put",
    )(*blocks, *extra)


def cut_kernel(places, part, block_ref, *refs):
    me = lax.axis_index("grp")
    outs, (in_sems, out_sems) = refs[: len(places)], refs[-2:]
    through = refs[len(places) : -2]
    copies = []
    for n, (k, row, size) in enumerate(places):
        offset = row if k is None else (me ^ k) * part + row
        held = through[n] if through else outs[n]
        copies.append(pltpu.make_async_copy(block_ref.at[pl.ds(offset, size), :], held, in_sems.at[n]))
        copies[n].start()
    for copy in copies:
        copy.wait()
    moves = [pltpu.make_async_copy(held, out, out_sems.at[n]) for n, (held, out) in enumerate(zip(through, outs))]
    for move in moves:
        move.start()
    for move in moves:
        move.wait()


def cut(block, places, part, fast):
    out = pltpu.VMEM if fast else pltpu.HBM
    through = [] if fast else [pltpu.VMEM((size, LANES), jnp.float32) for _, _, size in places]
    return pl.pallas_call(
        functools.partial(cut_kernel, places, part),
        out_shape=[out((size, LANES), jnp.float32) for _, _, size in places],
        in_specs=[HBM_SPEC],
        out_specs=[VMEM_SPEC if fast else HBM_SPEC] * len(places),
        scratch_shapes=through + [pltpu.SemaphoreType.DMA((len(places),))] * 2,
        compiler_params=pltpu.CompilerParams(vmem_limit_bytes=VMEM_LIMIT),
        cost_estimate=SHORT,
        name="cut",
    )(in_hbm(block))


def shards(particles, scores, kernel_width):
    groups = lax.axis_size("grp")
    rows = particles.shape[0]
    count = rows * groups
    x, s = dense(particles), dense(scores)
    part, half = x.shape[0] // groups, x.shape[0] // 2
    near = 2 ** ((groups.bit_length() - 1) // 2)
    lows, highs = list(range(near)), list(range(0, groups, near))

    def swap(block, k, axis="grp"):
        return lax.ppermute(block, axis, [(i, i ^ k) for i in range(lax.axis_size(axis))]) if k else block

    def stages(axis):
        left, step = lax.axis_size(axis), 1
        while left > 1:
            radix = 4 if left % 4 == 0 else 2
            yield [step * k for k in range(radix)]
            left, step = left // radix, step * radix

    everyone = list(range(groups))
    direct = [k for k in everyone[1:] if k in lows or k in highs]
    distant = [k for k in everyone[1:] if k not in direct]
    size, step = x.shape[0], SUB * rows
    first = max(1, half // step * 7 // 16) * step
    split = part // step // 2 * step
    halves = [(0, split), (split, part - split)]

    def legs(k, n):
        low, high = k % near, k - k % near
        return (low, high) if n == 0 else (high, low)

    def pieces(k):
        return halves if k in distant else [(0, part)]

    order = direct + distant
    sent = cut(x, [(k, 0, part) for k in order], part, True)
    s, sent = lax.optimization_barrier((s, sent))
    bounds = [(n * half + row, length) for n in (0, 1) for row, length in ((0, first), (first, half - first))]
    s_own = cut(s, [(None, *bound) for bound in bounds], part, False)
    xs = {k: swap(block, k) for k, block in zip(order, sent)}
    xs[order[0]], x, s_own = lax.optimization_barrier((xs[order[0]], x, s_own))
    xs[0] = cut(x, [(0, 0, part)], part, True)[0]
    xs = [[xs[k]] for k in everyone]

    def exchange(block, partners):
        return [swap(block, k) for k in partners]

    early = [exchange(s_own[0], lows), exchange(s_own[2], highs)]
    grams = [gram(xs, rows)]
    pair = [s_own[1], s_own[3]]
    for partners in stages("grp"):
        total = add(grams) if len(grams) > 1 else grams[0]
        grams = [swap(total, k) for k in partners]
    early, pair, grams = lax.optimization_barrier((early, pair, grams))
    late = [exchange(pair[0], lows), exchange(pair[1], highs)]
    for partners in stages("par"):
        grams = [swap(add(grams), k, "par") for k in partners]
    coefs = weights(kernel_width, grams, rows, count)

    s = in_hbm(s)

    def send(dest, jobs, coefs):
        mixed = mix(coefs, rows, count, jobs)
        return swap(mixed, dest), lax.optimization_barrier((coefs, mixed))[0]

    def particle_jobs(dest, start, length):
        jobs = []
        for n, (row, piece) in enumerate(halves):
            begin, extent = max(start, row), min(start + length, row + piece) - max(start, row)
            if extent > 0:
                blocks = [(xs[k][n], begin - row, extent, False) if len(xs[k]) > 1 else (xs[k][0], begin, extent, False) for k in everyone]
                jobs.append((True, dest, everyone, blocks))
        return jobs

    def score_jobs(dest, n, low, high):
        jobs = []
        for held, start, end in ((early, 0, first), (late, first, half)):
            begin, extent = max(low, start), min(high, end) - max(low, start)
            if extent > 0:
                blocks = [(s, n * half + begin, extent, True)] + [(block, begin - start, extent, True) for block in held[n][1:]]
                jobs.append((False, dest, (lows, highs)[n], blocks))
        return jobs

    back, sums = {}, {}
    for k in direct:
        back[k, 0], coefs = send(k, particle_jobs(k, 0, part), coefs)
    for k in distant:
        for n in (1, 0):
            hop, coefs = send(legs(k, n)[0], particle_jobs(k, *halves[n]), coefs)
            back[k, n] = swap(hop, legs(k, n)[1])
    middle = half // step // 2 * step
    spans = [span for span in ((0, middle), (middle, half)) if span[0] < span[1]]
    for span in spans:
        for n, dests in enumerate((highs[1:], lows[1:])):
            for k in dests:
                sums[span, k], coefs = send(k, score_jobs(k, n, *span), coefs)
    own_jobs = particle_jobs(0, 0, part)
    for span in spans:
        own_jobs += score_jobs(0, 0, *span) + score_jobs(0, 1, *span)
    own = mix(coefs, rows, count, own_jobs)

    def place(k):
        return [([(n, 0)], length, (k, row)) for n, (row, length) in enumerate(pieces(k))]

    repel = put([([(0, 0)], part, (0, 0))], [own], part, size)
    for k in direct:
        repel, got = lax.optimization_barrier((repel, back[k, 0]))
        repel = put(place(k), [got], part, size, base=repel)
    drive = None
    begin = part
    for span in spans:
        length = span[1] - span[0]
        for n, dests in enumerate((highs[1:], lows[1:])):
            got = [sums[span, k] for k in dests]
            held = repel if drive is None else (drive, repel)
            held, got = lax.optimization_barrier((held, got))
            drive, repel = (None, held) if drive is None else held
            entry = ([(0, begin)] + [(1 + m, 0) for m in range(len(got))], length, (None, n * half + span[0]))
            drive = put([entry], [own, *got], part, size, base=drive)
            begin += length
    for k in distant:
        got = [back[k, n] for n in (0, 1)]
        (drive, repel), got = lax.optimization_barrier(((drive, repel), got))
        repel = put(place(k), got, part, size, base=repel)
    return (undense(drive, rows), undense(repel, rows))


def solution(mesh):
    return jax.shard_map(
        shards,
        mesh=mesh,
        in_specs=(P("grp", "par"), P("grp", "par"), P()),
        out_specs=(P("grp", "par"), P("grp", "par")),
        check_vma=False,
    )
```

```python
import functools

import jax
import jax.numpy as jnp
from jax import lax
from jax.experimental import pallas as pl
from jax.experimental.pallas import tpu as pltpu
from jax.sharding import PartitionSpec as P

P_SIZE = 1048576
LANES = 128
SUB = 8
VMEM_LIMIT = 16 * 2**20

SMEM_SPEC = pl.BlockSpec(memory_space=pltpu.SMEM)
VMEM_SPEC = pl.BlockSpec(memory_space=pltpu.VMEM)
ANY_SPEC = pl.BlockSpec(memory_space=pl.ANY)
HBM_SPEC = pl.BlockSpec(memory_space=pltpu.HBM)
SHORT = pl.CostEstimate(flops=1, bytes_accessed=1, transcendentals=0)


def in_hbm(array):
    return pltpu.with_memory_space_constraint(array, pltpu.HBM)


def in_vmem(array):
    return pltpu.with_memory_space_constraint(array, pltpu.VMEM)


def dense(block):
    rows, columns = block.shape
    return block.reshape(rows, columns // LANES, LANES).transpose(1, 0, 2).reshape(-1, LANES)


def undense(block, rows):
    return block.reshape(-1, rows, LANES).transpose(1, 0, 2).reshape(rows, -1)


def gram_kernel(rows, groups, pairs, *refs):
    xs, (out_ref, acc_ref) = refs[:groups], refs[-2:]
    base = refs[groups : -2]
    me = lax.axis_index("grp")
    count = rows * groups
    step = SUB * rows
    steps = xs[0].shape[0] // step

    def load(ref, t, i):
        return ref[pl.ds(t * step + i, SUB, stride=rows), :]

    if len(pairs) < groups * (groups + 1) // 2:
        acc_ref[...] = jnp.zeros_like(acc_ref)
    for a, b in pairs:
        terms = [(i, j) for i in range(rows) for j in range(rows) if a != b or i <= j]

        def body(t, sums):
            left = [load(xs[a], t, i) for i in range(rows)]
            right = left if a == b else [load(xs[b], t, j) for j in range(rows)]
            return tuple(s + left[i] * right[j] for s, (i, j) in zip(sums, terms))

        sums = (jnp.zeros((SUB, LANES), jnp.float32),) * len(terms)
        sums = lax.fori_loop(0, steps, body, sums, unroll=2)
        for s, (i, j) in zip(sums, terms):
            row = jnp.sum(s, axis=0, keepdims=True)
            left, right = (me ^ a) * rows + i, (me ^ b) * rows + j
            acc_ref[pl.ds(left * count + right, 1), :] = row
            if a != b or i != j:
                acc_ref[pl.ds(right * count + left, 1), :] = row
    total = lax.dot_general(
        jnp.ones((SUB, LANES), jnp.float32),
        acc_ref[...],
        (((1,), (1,)), ((), ())),
        precision=lax.Precision.HIGHEST,
        preferred_element_type=jnp.float32,
    )
    for n in range(count * count // LANES):
        row = total[:1, n * LANES : (n + 1) * LANES]
        out_ref[:, n : n + 1, :] = (row + base[0][0, n : n + 1, :] if base else row)[None]


def gram(xs, rows, groups, pairs, base=None):
    count = rows * groups
    held = [xs.get(k, xs[0]) for k in range(groups)]
    extra = [] if base is None else [base]
    return pl.pallas_call(
        functools.partial(gram_kernel, rows, groups, pairs),
        out_shape=jax.ShapeDtypeStruct((1, count * count // LANES, LANES), jnp.float32),
        in_specs=[VMEM_SPEC] * (groups + len(extra)),
        out_specs=VMEM_SPEC,
        scratch_shapes=[pltpu.VMEM((count * count, LANES), jnp.float32)],
        compiler_params=pltpu.CompilerParams(vmem_limit_bytes=VMEM_LIMIT),
        cost_estimate=SHORT,
        name="gram",
    )(*map(in_vmem, held + extra))


def add_kernel(*refs):
    refs[-1][...] = sum((ref[...] for ref in refs[1:-1]), refs[0][...])


def add(blocks):
    return pl.pallas_call(
        add_kernel,
        out_shape=jax.ShapeDtypeStruct(blocks[0].shape, blocks[0].dtype),
        in_specs=[VMEM_SPEC] * len(blocks),
        out_specs=VMEM_SPEC,
        compiler_params=pltpu.CompilerParams(vmem_limit_bytes=2**21),
        cost_estimate=SHORT,
        name="add",
    )(*blocks)


def exact(left, right):
    return jnp.dot(left, right, precision=lax.Precision.HIGHEST, preferred_element_type=jnp.float32)


def weights_kernel(rows, count, width_ref, *refs):
    me = lax.axis_index("grp")
    grams, drive_ref, repel_ref = refs[:-2], refs[-2], refs[-1]

    def iota(shape, axis):
        return lax.broadcasted_iota(jnp.int32, shape, axis)

    def mask(condition):
        return jnp.where(condition, 1.0, 0.0)

    flat = sum((ref[0] for ref in grams[1:]), grams[0][0])
    lines = flat.shape[0]
    per = LANES // count
    held = exact(mask(iota((count, lines), 0) // per == iota((count, lines), 1)), flat)
    held = jnp.where(iota((count, LANES), 1) // count == iota((count, LANES), 0) % per, held, 0.0)
    inner = exact(held, mask(iota((LANES, count), 0) % count == iota((LANES, count), 1)))
    square = (count, count)
    r, c = iota(square, 0), iota(square, 1)
    order = mask(((me ^ (r // rows)) * rows + r % rows) == c)
    inner = exact(exact(order, inner), order)

    width = width_ref[0]
    diagonal = r == c
    norms = jnp.where(diagonal, inner, 0.0)
    dist = jnp.sum(norms, axis=1, keepdims=True) + jnp.sum(norms, axis=0, keepdims=True) - 2.0 * inner
    kern = jnp.exp(-dist / (width * P_SIZE))
    others = jnp.where(diagonal, 0.0, kern)
    to_drive = kern / count
    to_repel = jnp.where(diagonal, jnp.sum(others, axis=1, keepdims=True), -others) / (count * width)
    for j in range(count):
        drive_ref[j * count : (j + 1) * count, :] = jnp.broadcast_to(to_drive[:, j : j + 1], (count, LANES))
        repel_ref[j * count : (j + 1) * count, :] = jnp.broadcast_to(to_repel[:, j : j + 1], (count, LANES))


def weights(width, grams, rows, count):
    shape = jax.ShapeDtypeStruct((count * count, LANES), jnp.float32)
    return pl.pallas_call(
        functools.partial(weights_kernel, rows, count),
        out_shape=(shape, shape),
        in_specs=[SMEM_SPEC] + [VMEM_SPEC] * len(grams),
        out_specs=(VMEM_SPEC, VMEM_SPEC),
        compiler_params=pltpu.CompilerParams(vmem_limit_bytes=VMEM_LIMIT),
        cost_estimate=SHORT,
        name="weights",
    )(width, *grams)


def mix_kernel(rows, count, jobs, drive_ref, repel_ref, *refs):
    spans = [span for job in jobs for span in job[3]]
    xs, out_ref, scratch = list(refs[: len(spans)]), refs[len(spans)], refs[len(spans) + 1 :]
    offsets = [start for start, _, _ in spans]
    copies = {}
    for n, (start, size, stream) in enumerate(spans):
        if stream:
            m = len(copies)
            copies[n] = pltpu.make_async_copy(xs[n].at[pl.ds(start, size), :], scratch[m], scratch[-1].at[m])
            copies[n].start()
            xs[n], offsets[n] = scratch[m], 0
    step = SUB * rows
    done = used = 0
    for repel, dest, sources, spans in jobs:
        coef_ref = repel_ref if repel else drive_ref
        held = [(xs[n], offsets[n]) for n in range(used, used + len(sources))]
        for n in range(used, used + len(sources)):
            if n in copies:
                copies[n].wait()
        used += len(sources)
        steps = spans[0][1] // step
        wide = next(w for w in (8, 4, 2, 1) if steps % w == 0)

        def body(t, carry):
            base = pl.multiple_of(t * step * wide, step)
            sums = [[None] * rows for _ in range(wide)]
            for (ref, offset), source in zip(held, sources):
                for j in range(rows):
                    x = [ref[pl.ds(offset + base + u * step + j, SUB, stride=rows), :] for u in range(wide)]
                    for i in range(rows):
                        row = (source * rows + j) * count + dest * rows + i
                        c = jnp.broadcast_to(coef_ref[row : row + 1, :], (SUB, LANES))
                        for u in range(wide):
                            term = c * x[u]
                            sums[u][i] = term if sums[u][i] is None else sums[u][i] + term
            for u in range(wide):
                for i in range(rows):
                    out_ref[pl.ds(done + base + u * step + i, SUB, stride=rows), :] = sums[u][i]
            return carry

        lax.fori_loop(0, steps // wide, body, 0)
        done += steps * step


def mix(coefs, rows, count, jobs):
    blocks = [block for job in jobs for block in job[3]]
    streams = [block for block in blocks if block[3]]
    return pl.pallas_call(
        functools.partial(mix_kernel, rows, count, [(*job[:3], [block[1:] for block in job[3]]) for job in jobs]),
        out_shape=jax.ShapeDtypeStruct((sum(job[3][0][2] for job in jobs), LANES), jnp.float32),
        in_specs=[VMEM_SPEC] * 2 + [ANY_SPEC if block[3] else VMEM_SPEC for block in blocks],
        out_specs=VMEM_SPEC,
        scratch_shapes=[pltpu.VMEM((block[2], LANES), jnp.float32) for block in streams]
        + ([pltpu.SemaphoreType.DMA((len(streams),))] if streams else []),
        compiler_params=pltpu.CompilerParams(vmem_limit_bytes=VMEM_LIMIT),
        cost_estimate=SHORT,
        name="mix",
    )(*coefs, *[block[0] if block[3] else in_vmem(block[0]) for block in blocks])


def put_kernel(entries, part, blocks, *refs):
    me = lax.axis_index("grp")
    blocks, (out_ref, sum_ref, sems) = refs[:blocks], refs[-3:]
    copies = []
    used = 0
    for n, (parts, size, (k, row)) in enumerate(entries):
        block, start = parts[0]
        source = blocks[block].at[pl.ds(start, size), :]
        if len(parts) > 1:
            total = source[...]
            for block, start in parts[1:]:
                total = total + blocks[block][pl.ds(start, size), :]
            source = sum_ref.at[pl.ds(used, size), :]
            source[...] = total
            used += size
        offset = row if k is None else (me ^ k) * part + row
        copy = pltpu.make_async_copy(source, out_ref.at[pl.ds(offset, size), :], sems.at[n])
        copy.start()
        copies.append(copy)
    for copy in copies:
        copy.wait()


def put(entries, blocks, part, size, base=None):
    extra = [] if base is None else [base]
    moved = sum(entry[1] for entry in entries)
    scratch = sum(entry[1] for entry in entries if len(entry[0]) > 1)
    return pl.pallas_call(
        functools.partial(put_kernel, entries, part, len(blocks)),
        out_shape=jax.ShapeDtypeStruct((size, LANES), jnp.float32),
        in_specs=[VMEM_SPEC] * len(blocks) + [HBM_SPEC] * len(extra),
        out_specs=HBM_SPEC,
        scratch_shapes=[pltpu.VMEM((max(scratch, SUB), LANES), jnp.float32), pltpu.SemaphoreType.DMA((len(entries),))],
        input_output_aliases={len(blocks): 0} if extra else {},
        compiler_params=pltpu.CompilerParams(vmem_limit_bytes=VMEM_LIMIT),
        cost_estimate=pl.CostEstimate(flops=0, bytes_accessed=8 * LANES * moved, transcendentals=0),
        name="put",
    )(*blocks, *extra)


def cut_kernel(places, part, block_ref, *refs):
    me = lax.axis_index("grp")
    outs, (in_sems, out_sems) = refs[: len(places)], refs[-2:]
    through = refs[len(places) : -2]
    copies = []
    for n, (k, row, size) in enumerate(places):
        offset = row if k is None else (me ^ k) * part + row
        held = through[n] if through else outs[n]
        copies.append(pltpu.make_async_copy(block_ref.at[pl.ds(offset, size), :], held, in_sems.at[n]))
        copies[n].start()
    for copy in copies:
        copy.wait()
    moves = [pltpu.make_async_copy(held, out, out_sems.at[n]) for n, (held, out) in enumerate(zip(through, outs))]
    for move in moves:
        move.start()
    for move in moves:
        move.wait()


def cut(block, places, part, fast):
    out = pltpu.VMEM if fast else pltpu.HBM
    through = [] if fast else [pltpu.VMEM((size, LANES), jnp.float32) for _, _, size in places]
    return pl.pallas_call(
        functools.partial(cut_kernel, places, part),
        out_shape=[out((size, LANES), jnp.float32) for _, _, size in places],
        in_specs=[HBM_SPEC],
        out_specs=[VMEM_SPEC if fast else HBM_SPEC] * len(places),
        scratch_shapes=through + [pltpu.SemaphoreType.DMA((len(places),))] * 2,
        compiler_params=pltpu.CompilerParams(vmem_limit_bytes=VMEM_LIMIT),
        cost_estimate=SHORT,
        name="cut",
    )(in_hbm(block))


def shards(particles, scores, kernel_width):
    groups = lax.axis_size("grp")
    rows = particles.shape[0]
    count = rows * groups
    x, s = dense(particles), dense(scores)
    part, half = x.shape[0] // groups, x.shape[0] // 2
    near = 2 ** ((groups.bit_length() - 1) // 2)
    lows, highs = list(range(near)), list(range(0, groups, near))

    def swap(block, k, axis="grp"):
        return lax.ppermute(block, axis, [(i, i ^ k) for i in range(lax.axis_size(axis))]) if k else block

    def stages(axis):
        left, step = lax.axis_size(axis), 1
        while left > 1:
            radix = 4 if left % 4 == 0 else 2
            yield [step * k for k in range(radix)]
            left, step = left // radix, step * radix

    everyone = list(range(groups))
    direct = [k for k in everyone[1:] if k in lows or k in highs]
    distant = [k for k in everyone[1:] if k not in direct]
    size, step = x.shape[0], SUB * rows
    first = max(1, half // step * 7 // 16) * step
    split = part // step // 2 * step
    halves = [(0, split), (split, part - split)]

    def legs(k, n):
        low, high = k % near, k - k % near
        return (low, high) if n == 0 else (high, low)

    def pieces(k):
        return halves if k in distant else [(0, part)]

    order = direct + distant
    sent = cut(x, [(k, 0, part) for k in order], part, True)
    s, sent = lax.optimization_barrier((s, sent))
    bounds = [(n * half + row, length) for n in (0, 1) for row, length in ((0, first), (first, half - first))]
    s_own = cut(s, [(None, *bound) for bound in bounds], part, False)
    xs = {k: swap(block, k) for k, block in zip(order, sent)}
    xs[order[0]], x, s_own = lax.optimization_barrier((xs[order[0]], x, s_own))
    xs[0] = cut(x, [(0, 0, part)], part, True)[0]
    pairs = [(a, b) for a in everyone for b in everyone if a <= b]
    late_pairs = [pair for pair in pairs if pair[0] in distant or pair[1] in distant]
    inner = gram({k: xs[k] for k in [0] + direct}, rows, groups, [pair for pair in pairs if pair not in late_pairs])
    if late_pairs:
        inner = gram(xs, rows, groups, late_pairs, inner)
    xs = [[xs[k]] for k in everyone]

    def exchange(block, partners):
        return [swap(block, k) for k in partners]

    early = [exchange(s_own[0], lows), exchange(s_own[2], highs)]
    grams = [inner]
    pair = [s_own[1], s_own[3]]
    for partners in stages("grp"):
        total = add(grams) if len(grams) > 1 else grams[0]
        grams = [swap(total, k) for k in partners]
    early, pair, grams = lax.optimization_barrier((early, pair, grams))
    late = [exchange(pair[0], lows), exchange(pair[1], highs)]
    for partners in stages("par"):
        grams = [swap(add(grams), k, "par") for k in partners]
    coefs = weights(kernel_width, grams, rows, count)

    s = in_hbm(s)

    def send(dest, jobs, coefs):
        mixed = mix(coefs, rows, count, jobs)
        return swap(mixed, dest), lax.optimization_barrier((coefs, mixed))[0]

    def particle_jobs(dest, start, length):
        jobs = []
        for n, (row, piece) in enumerate(halves):
            begin, extent = max(start, row), min(start + length, row + piece) - max(start, row)
            if extent > 0:
                blocks = [(xs[k][n], begin - row, extent, False) if len(xs[k]) > 1 else (xs[k][0], begin, extent, False) for k in everyone]
                jobs.append((True, dest, everyone, blocks))
        return jobs

    def score_jobs(dest, n, low, high):
        jobs = []
        for held, start, end in ((early, 0, first), (late, first, half)):
            begin, extent = max(low, start), min(high, end) - max(low, start)
            if extent > 0:
                blocks = [(s, n * half + begin, extent, True)] + [(block, begin - start, extent, True) for block in held[n][1:]]
                jobs.append((False, dest, (lows, highs)[n], blocks))
        return jobs

    back, sums = {}, {}
    for k in direct:
        back[k, 0], coefs = send(k, particle_jobs(k, 0, part), coefs)
    for k in distant:
        for n in (1, 0):
            hop, coefs = send(legs(k, n)[0], particle_jobs(k, *halves[n]), coefs)
            back[k, n] = swap(hop, legs(k, n)[1])
    middle = half // step // 2 * step
    spans = [span for span in ((0, middle), (middle, half)) if span[0] < span[1]]
    for span in spans:
        for n, dests in enumerate((highs[1:], lows[1:])):
            for k in dests:
                sums[span, k], coefs = send(k, score_jobs(k, n, *span), coefs)
    own_jobs = particle_jobs(0, 0, part)
    for span in spans:
        own_jobs += score_jobs(0, 0, *span) + score_jobs(0, 1, *span)
    own = mix(coefs, rows, count, own_jobs)

    def place(k):
        return [([(n, 0)], length, (k, row)) for n, (row, length) in enumerate(pieces(k))]

    repel = put([([(0, 0)], part, (0, 0))], [own], part, size)
    for k in direct:
        repel, got = lax.optimization_barrier((repel, back[k, 0]))
        repel = put(place(k), [got], part, size, base=repel)
    drive = None
    begin = part
    for span in spans:
        length = span[1] - span[0]
        for n, dests in enumerate((highs[1:], lows[1:])):
            got = [sums[span, k] for k in dests]
            held = repel if drive is None else (drive, repel)
            held, got = lax.optimization_barrier((held, got))
            drive, repel = (None, held) if drive is None else held
            entry = ([(0, begin)] + [(1 + m, 0) for m in range(len(got))], length, (None, n * half + span[0]))
            drive = put([entry], [own, *got], part, size, base=drive)
            begin += length
    for k in distant:
        got = [back[k, n] for n in (0, 1)]
        (drive, repel), got = lax.optimization_barrier(((drive, repel), got))
        repel = put(place(k), got, part, size, base=repel)
    return (undense(drive, rows), undense(repel, rows))


def solution(mesh):
    return jax.shard_map(
        shards,
        mesh=mesh,
        in_specs=(P("grp", "par"), P("grp", "par"), P()),
        out_specs=(P("grp", "par"), P("grp", "par")),
        check_vma=False,
    )
```

```python
import functools

import jax
import jax.numpy as jnp
from jax import lax
from jax.experimental import pallas as pl
from jax.experimental.pallas import tpu as pltpu
from jax.sharding import PartitionSpec as P

P_SIZE = 1048576
LANES = 128
SUB = 8
VMEM_LIMIT = 16 * 2**20

SMEM_SPEC = pl.BlockSpec(memory_space=pltpu.SMEM)
VMEM_SPEC = pl.BlockSpec(memory_space=pltpu.VMEM)
ANY_SPEC = pl.BlockSpec(memory_space=pl.ANY)
HBM_SPEC = pl.BlockSpec(memory_space=pltpu.HBM)
SHORT = pl.CostEstimate(flops=1, bytes_accessed=1, transcendentals=0)


def in_hbm(array):
    return pltpu.with_memory_space_constraint(array, pltpu.HBM)


def in_vmem(array):
    return pltpu.with_memory_space_constraint(array, pltpu.VMEM)


def dense(block):
    rows, columns = block.shape
    return block.reshape(rows, columns // LANES, LANES).transpose(1, 0, 2).reshape(-1, LANES)


def undense(block, rows):
    return block.reshape(-1, rows, LANES).transpose(1, 0, 2).reshape(rows, -1)


def gram_kernel(rows, pieces, *refs):
    out_ref, acc_ref = refs[-2], refs[-1]
    me = lax.axis_index("grp")
    groups, count = len(pieces), rows * len(pieces)
    step = SUB * rows
    xs = [refs[sum(pieces[:k]) : sum(pieces[: k + 1])] for k in range(groups)]
    cuts = max(pieces)
    steps = sum(x.shape[0] for x in xs[0]) // step // cuts

    def load(x, cut, t, i):
        ref, base = (x[cut], 0) if len(x) > 1 else (x[0], cut * steps * step)
        return ref[pl.ds(base + t * step + i, SUB, stride=rows), :]

    for a in range(groups):
        for b in range(a, groups):
            pairs = [(i, j) for i in range(rows) for j in range(rows) if a != b or i <= j]
            sums = (jnp.zeros((SUB, LANES), jnp.float32),) * len(pairs)
            for cut in range(cuts):

                def body(t, sums):
                    left = [load(xs[a], cut, t, i) for i in range(rows)]
                    right = left if a == b else [load(xs[b], cut, t, j) for j in range(rows)]
                    return tuple(s + left[i] * right[j] for s, (i, j) in zip(sums, pairs))

                sums = lax.fori_loop(0, steps, body, sums, unroll=2)
            for s, (i, j) in zip(sums, pairs):
                row = jnp.sum(s, axis=0, keepdims=True)
                left, right = (me ^ a) * rows + i, (me ^ b) * rows + j
                acc_ref[pl.ds(left * count + right, 1), :] = row
                if a != b or i != j:
                    acc_ref[pl.ds(right * count + left, 1), :] = row
    total = lax.dot_general(
        jnp.ones((SUB, LANES), jnp.float32),
        acc_ref[...],
        (((1,), (1,)), ((), ())),
        precision=lax.Precision.HIGHEST,
        preferred_element_type=jnp.float32,
    )
    for n in range(count * count // LANES):
        row = total[:1, n * LANES : (n + 1) * LANES]
        out_ref[:, n : n + 1, :] = row[None]


def gram(xs, rows):
    blocks = [block for x in xs for block in x]
    count = rows * len(xs)
    return pl.pallas_call(
        functools.partial(gram_kernel, rows, [len(x) for x in xs]),
        out_shape=jax.ShapeDtypeStruct((1, count * count // LANES, LANES), jnp.float32),
        in_specs=[VMEM_SPEC] * len(blocks),
        out_specs=VMEM_SPEC,
        scratch_shapes=[pltpu.VMEM((count * count, LANES), jnp.float32)],
        compiler_params=pltpu.CompilerParams(vmem_limit_bytes=VMEM_LIMIT),
        cost_estimate=SHORT,
        name="gram",
    )(*map(in_vmem, blocks))


def add_kernel(*refs):
    refs[-1][...] = sum((ref[...] for ref in refs[1:-1]), refs[0][...])


def add(blocks):
    return pl.pallas_call(
        add_kernel,
        out_shape=jax.ShapeDtypeStruct(blocks[0].shape, blocks[0].dtype),
        in_specs=[VMEM_SPEC] * len(blocks),
        out_specs=VMEM_SPEC,
        compiler_params=pltpu.CompilerParams(vmem_limit_bytes=2**21),
        cost_estimate=SHORT,
        name="add",
    )(*blocks)


def exact(left, right):
    return jnp.dot(left, right, precision=lax.Precision.HIGHEST, preferred_element_type=jnp.float32)


def weights_kernel(rows, count, width_ref, *refs):
    me = lax.axis_index("grp")
    grams, drive_ref, repel_ref = refs[:-2], refs[-2], refs[-1]

    def iota(shape, axis):
        return lax.broadcasted_iota(jnp.int32, shape, axis)

    def mask(condition):
        return jnp.where(condition, 1.0, 0.0)

    flat = sum((ref[0] for ref in grams[1:]), grams[0][0])
    lines = flat.shape[0]
    per = LANES // count
    held = exact(mask(iota((count, lines), 0) // per == iota((count, lines), 1)), flat)
    held = jnp.where(iota((count, LANES), 1) // count == iota((count, LANES), 0) % per, held, 0.0)
    inner = exact(held, mask(iota((LANES, count), 0) % count == iota((LANES, count), 1)))
    square = (count, count)
    r, c = iota(square, 0), iota(square, 1)
    order = mask(((me ^ (r // rows)) * rows + r % rows) == c)
    inner = exact(exact(order, inner), order)

    width = width_ref[0]
    diagonal = r == c
    norms = jnp.where(diagonal, inner, 0.0)
    dist = jnp.sum(norms, axis=1, keepdims=True) + jnp.sum(norms, axis=0, keepdims=True) - 2.0 * inner
    kern = jnp.exp(-dist / (width * P_SIZE))
    others = jnp.where(diagonal, 0.0, kern)
    to_drive = kern / count
    to_repel = jnp.where(diagonal, jnp.sum(others, axis=1, keepdims=True), -others) / (count * width)
    for j in range(count):
        drive_ref[j * count : (j + 1) * count, :] = jnp.broadcast_to(to_drive[:, j : j + 1], (count, LANES))
        repel_ref[j * count : (j + 1) * count, :] = jnp.broadcast_to(to_repel[:, j : j + 1], (count, LANES))


def weights(width, grams, rows, count):
    shape = jax.ShapeDtypeStruct((count * count, LANES), jnp.float32)
    return pl.pallas_call(
        functools.partial(weights_kernel, rows, count),
        out_shape=(shape, shape),
        in_specs=[SMEM_SPEC] + [VMEM_SPEC] * len(grams),
        out_specs=(VMEM_SPEC, VMEM_SPEC),
        compiler_params=pltpu.CompilerParams(vmem_limit_bytes=VMEM_LIMIT),
        cost_estimate=SHORT,
        name="weights",
    )(width, *grams)


def mix_kernel(rows, count, jobs, drive_ref, repel_ref, *refs):
    spans = [span for job in jobs for span in job[3]]
    xs, out_ref, scratch = list(refs[: len(spans)]), refs[len(spans)], refs[len(spans) + 1 :]
    offsets = [start for start, _, _ in spans]
    copies = {}
    for n, (start, size, stream) in enumerate(spans):
        if stream:
            m = len(copies)
            copies[n] = pltpu.make_async_copy(xs[n].at[pl.ds(start, size), :], scratch[m], scratch[-1].at[m])
            copies[n].start()
            xs[n], offsets[n] = scratch[m], 0
    step = SUB * rows
    done = used = 0
    for repel, dest, sources, spans in jobs:
        coef_ref = repel_ref if repel else drive_ref
        held = [(xs[n], offsets[n]) for n in range(used, used + len(sources))]
        for n in range(used, used + len(sources)):
            if n in copies:
                copies[n].wait()
        used += len(sources)
        steps = spans[0][1] // step
        wide = next(w for w in (8, 4, 2, 1) if steps % w == 0)

        def body(t, carry):
            base = pl.multiple_of(t * step * wide, step)
            sums = [[None] * rows for _ in range(wide)]
            for (ref, offset), source in zip(held, sources):
                for j in range(rows):
                    x = [ref[pl.ds(offset + base + u * step + j, SUB, stride=rows), :] for u in range(wide)]
                    for i in range(rows):
                        row = (source * rows + j) * count + dest * rows + i
                        c = jnp.broadcast_to(coef_ref[row : row + 1, :], (SUB, LANES))
                        for u in range(wide):
                            term = c * x[u]
                            sums[u][i] = term if sums[u][i] is None else sums[u][i] + term
            for u in range(wide):
                for i in range(rows):
                    out_ref[pl.ds(done + base + u * step + i, SUB, stride=rows), :] = sums[u][i]
            return carry

        lax.fori_loop(0, steps // wide, body, 0)
        done += steps * step


def mix(coefs, rows, count, jobs):
    blocks = [block for job in jobs for block in job[3]]
    streams = [block for block in blocks if block[3]]
    return pl.pallas_call(
        functools.partial(mix_kernel, rows, count, [(*job[:3], [block[1:] for block in job[3]]) for job in jobs]),
        out_shape=jax.ShapeDtypeStruct((sum(job[3][0][2] for job in jobs), LANES), jnp.float32),
        in_specs=[VMEM_SPEC] * 2 + [ANY_SPEC if block[3] else VMEM_SPEC for block in blocks],
        out_specs=VMEM_SPEC,
        scratch_shapes=[pltpu.VMEM((block[2], LANES), jnp.float32) for block in streams]
        + ([pltpu.SemaphoreType.DMA((len(streams),))] if streams else []),
        compiler_params=pltpu.CompilerParams(vmem_limit_bytes=VMEM_LIMIT),
        cost_estimate=SHORT,
        name="mix",
    )(*coefs, *[block[0] if block[3] else in_vmem(block[0]) for block in blocks])


def put_kernel(entries, part, blocks, *refs):
    me = lax.axis_index("grp")
    blocks, (out_ref, sum_ref, sems) = refs[:blocks], refs[-3:]
    copies = []
    used = 0
    for n, (parts, size, (k, row)) in enumerate(entries):
        block, start = parts[0]
        source = blocks[block].at[pl.ds(start, size), :]
        if len(parts) > 1:
            total = source[...]
            for block, start in parts[1:]:
                total = total + blocks[block][pl.ds(start, size), :]
            source = sum_ref.at[pl.ds(used, size), :]
            source[...] = total
            used += size
        offset = row if k is None else (me ^ k) * part + row
        copy = pltpu.make_async_copy(source, out_ref.at[pl.ds(offset, size), :], sems.at[n])
        copy.start()
        copies.append(copy)
    for copy in copies:
        copy.wait()


def put(entries, blocks, part, size, base=None):
    extra = [] if base is None else [base]
    moved = sum(entry[1] for entry in entries)
    scratch = sum(entry[1] for entry in entries if len(entry[0]) > 1)
    return pl.pallas_call(
        functools.partial(put_kernel, entries, part, len(blocks)),
        out_shape=jax.ShapeDtypeStruct((size, LANES), jnp.float32),
        in_specs=[VMEM_SPEC] * len(blocks) + [HBM_SPEC] * len(extra),
        out_specs=HBM_SPEC,
        scratch_shapes=[pltpu.VMEM((max(scratch, SUB), LANES), jnp.float32), pltpu.SemaphoreType.DMA((len(entries),))],
        input_output_aliases={len(blocks): 0} if extra else {},
        compiler_params=pltpu.CompilerParams(vmem_limit_bytes=VMEM_LIMIT),
        cost_estimate=pl.CostEstimate(flops=0, bytes_accessed=8 * LANES * moved, transcendentals=0),
        name="put",
    )(*blocks, *extra)


def cut_kernel(places, part, block_ref, *refs):
    me = lax.axis_index("grp")
    outs, (in_sems, out_sems) = refs[: len(places)], refs[-2:]
    through = refs[len(places) : -2]
    copies = []
    for n, (k, row, size) in enumerate(places):
        offset = row if k is None else (me ^ k) * part + row
        held = through[n] if through else outs[n]
        copies.append(pltpu.make_async_copy(block_ref.at[pl.ds(offset, size), :], held, in_sems.at[n]))
        copies[n].start()
    for copy in copies:
        copy.wait()
    moves = [pltpu.make_async_copy(held, out, out_sems.at[n]) for n, (held, out) in enumerate(zip(through, outs))]
    for move in moves:
        move.start()
    for move in moves:
        move.wait()


def cut(block, places, part, fast):
    out = pltpu.VMEM if fast else pltpu.HBM
    through = [] if fast else [pltpu.VMEM((size, LANES), jnp.float32) for _, _, size in places]
    return pl.pallas_call(
        functools.partial(cut_kernel, places, part),
        out_shape=[out((size, LANES), jnp.float32) for _, _, size in places],
        in_specs=[HBM_SPEC],
        out_specs=[VMEM_SPEC if fast else HBM_SPEC] * len(places),
        scratch_shapes=through + [pltpu.SemaphoreType.DMA((len(places),))] * 2,
        compiler_params=pltpu.CompilerParams(vmem_limit_bytes=VMEM_LIMIT),
        cost_estimate=SHORT,
        name="cut",
    )(in_hbm(block))


def shards(particles, scores, kernel_width):
    groups = lax.axis_size("grp")
    rows = particles.shape[0]
    count = rows * groups
    x, s = dense(particles), dense(scores)
    part, half = x.shape[0] // groups, x.shape[0] // 2
    near = 2 ** ((groups.bit_length() - 1) // 2)
    lows, highs = list(range(near)), list(range(0, groups, near))

    def swap(block, k, axis="grp"):
        return lax.ppermute(block, axis, [(i, i ^ k) for i in range(lax.axis_size(axis))]) if k else block

    def stages(axis):
        left, step = lax.axis_size(axis), 1
        while left > 1:
            radix = 4 if left % 4 == 0 else 2
            yield [step * k for k in range(radix)]
            left, step = left // radix, step * radix

    everyone = list(range(groups))
    direct = [k for k in everyone[1:] if k in lows or k in highs]
    distant = [k for k in everyone[1:] if k not in direct]
    size, step = x.shape[0], SUB * rows
    first = max(1, half // step * 7 // 16) * step
    split = part // step // 2 * step
    halves = [(0, split), (split, part - split)]

    def legs(k, n):
        low, high = k % near, k - k % near
        return (low, high) if n == 0 else (high, low)

    def pieces(k):
        return halves if k in distant else [(0, part)]

    order = direct + distant
    sent = cut(x, [(k, 0, part) for k in order], part, True)
    s, sent = lax.optimization_barrier((s, sent))
    bounds = [(n * half + row, length) for n in (0, 1) for row, length in ((0, first), (first, half - first))]
    s_own = cut(s, [(None, *bound) for bound in bounds], part, True)
    xs = {k: swap(block, k) for k, block in zip(order, sent)}
    xs[order[0]], x, s_own = lax.optimization_barrier((xs[order[0]], x, s_own))
    xs[0] = cut(x, [(0, 0, part)], part, True)[0]
    xs = [[xs[k]] for k in everyone]

    def exchange(block, partners):
        return [swap(block, k) for k in partners]

    early = [exchange(s_own[0], lows), exchange(s_own[2], highs)]
    grams = [gram(xs, rows)]
    pair = [s_own[1], s_own[3]]
    for partners in stages("grp"):
        total = add(grams) if len(grams) > 1 else grams[0]
        grams = [swap(total, k) for k in partners]
    early, pair, grams = lax.optimization_barrier((early, pair, grams))
    late = [exchange(pair[0], lows), exchange(pair[1], highs)]
    for partners in stages("par"):
        grams = [swap(add(grams), k, "par") for k in partners]
    coefs = weights(kernel_width, grams, rows, count)

    s = in_hbm(s)

    def send(dest, jobs, coefs):
        mixed = mix(coefs, rows, count, jobs)
        return swap(mixed, dest), lax.optimization_barrier((coefs, mixed))[0]

    def particle_jobs(dest, start, length):
        jobs = []
        for n, (row, piece) in enumerate(halves):
            begin, extent = max(start, row), min(start + length, row + piece) - max(start, row)
            if extent > 0:
                blocks = [(xs[k][n], begin - row, extent, False) if len(xs[k]) > 1 else (xs[k][0], begin, extent, False) for k in everyone]
                jobs.append((True, dest, everyone, blocks))
        return jobs

    def score_jobs(dest, n, low, high):
        jobs = []
        for held, start, end in ((early, 0, first), (late, first, half)):
            begin, extent = max(low, start), min(high, end) - max(low, start)
            if extent > 0:
                blocks = [(s, n * half + begin, extent, True)] + [(block, begin - start, extent, True) for block in held[n][1:]]
                jobs.append((False, dest, (lows, highs)[n], blocks))
        return jobs

    back, sums = {}, {}
    for k in direct:
        back[k, 0], coefs = send(k, particle_jobs(k, 0, part), coefs)
    for k in distant:
        for n in (1, 0):
            hop, coefs = send(legs(k, n)[0], particle_jobs(k, *halves[n]), coefs)
            back[k, n] = swap(hop, legs(k, n)[1])
    middle = half // step // 2 * step
    spans = [span for span in ((0, middle), (middle, half)) if span[0] < span[1]]
    for span in spans:
        for n, dests in enumerate((highs[1:], lows[1:])):
            for k in dests:
                sums[span, k], coefs = send(k, score_jobs(k, n, *span), coefs)
    own_jobs = particle_jobs(0, 0, part)
    for span in spans:
        own_jobs += score_jobs(0, 0, *span) + score_jobs(0, 1, *span)
    own = mix(coefs, rows, count, own_jobs)

    def place(k):
        return [([(n, 0)], length, (k, row)) for n, (row, length) in enumerate(pieces(k))]

    repel = put([([(0, 0)], part, (0, 0))], [own], part, size)
    for k in direct:
        repel, got = lax.optimization_barrier((repel, back[k, 0]))
        repel = put(place(k), [got], part, size, base=repel)
    drive = None
    begin = part
    for span in spans:
        length = span[1] - span[0]
        for n, dests in enumerate((highs[1:], lows[1:])):
            got = [sums[span, k] for k in dests]
            held = repel if drive is None else (drive, repel)
            held, got = lax.optimization_barrier((held, got))
            drive, repel = (None, held) if drive is None else held
            entry = ([(0, begin)] + [(1 + m, 0) for m in range(len(got))], length, (None, n * half + span[0]))
            drive = put([entry], [own, *got], part, size, base=drive)
            begin += length
    for k in distant:
        got = [back[k, n] for n in (0, 1)]
        (drive, repel), got = lax.optimization_barrier(((drive, repel), got))
        repel = put(place(k), got, part, size, base=repel)
    return (undense(drive, rows), undense(repel, rows))


def solution(mesh):
    return jax.shard_map(
        shards,
        mesh=mesh,
        in_specs=(P("grp", "par"), P("grp", "par"), P()),
        out_specs=(P("grp", "par"), P("grp", "par")),
        check_vma=False,
    )
```

```python
import functools

import jax
import jax.numpy as jnp
from jax import lax
from jax.experimental import pallas as pl
from jax.experimental.pallas import tpu as pltpu
from jax.sharding import PartitionSpec as P

P_SIZE = 1048576
LANES = 128
SUB = 8
VMEM_LIMIT = 16 * 2**20

SMEM_SPEC = pl.BlockSpec(memory_space=pltpu.SMEM)
VMEM_SPEC = pl.BlockSpec(memory_space=pltpu.VMEM)
ANY_SPEC = pl.BlockSpec(memory_space=pl.ANY)
HBM_SPEC = pl.BlockSpec(memory_space=pltpu.HBM)
SHORT = pl.CostEstimate(flops=1, bytes_accessed=1, transcendentals=0)


def in_hbm(array):
    return pltpu.with_memory_space_constraint(array, pltpu.HBM)


def in_vmem(array):
    return pltpu.with_memory_space_constraint(array, pltpu.VMEM)


def dense(block):
    rows, columns = block.shape
    return block.reshape(rows, columns // LANES, LANES).transpose(1, 0, 2).reshape(-1, LANES)


def undense(block, rows):
    return block.reshape(-1, rows, LANES).transpose(1, 0, 2).reshape(rows, -1)


def gram_kernel(rows, groups, pairs, *refs):
    xs, (out_ref, acc_ref) = refs[:groups], refs[-2:]
    base = refs[groups : -2]
    me = lax.axis_index("grp")
    count = rows * groups
    step = SUB * rows
    steps = xs[0].shape[0] // step

    def load(ref, t, i):
        return ref[pl.ds(t * step + i, SUB, stride=rows), :]

    if len(pairs) < groups * (groups + 1) // 2:
        acc_ref[...] = jnp.zeros_like(acc_ref)
    for a, b in pairs:
        terms = [(i, j) for i in range(rows) for j in range(rows) if a != b or i <= j]

        def body(t, sums):
            left = [load(xs[a], t, i) for i in range(rows)]
            right = left if a == b else [load(xs[b], t, j) for j in range(rows)]
            return tuple(s + left[i] * right[j] for s, (i, j) in zip(sums, terms))

        sums = (jnp.zeros((SUB, LANES), jnp.float32),) * len(terms)
        sums = lax.fori_loop(0, steps, body, sums, unroll=2)
        for s, (i, j) in zip(sums, terms):
            row = jnp.sum(s, axis=0, keepdims=True)
            left, right = (me ^ a) * rows + i, (me ^ b) * rows + j
            acc_ref[pl.ds(left * count + right, 1), :] = row
            if a != b or i != j:
                acc_ref[pl.ds(right * count + left, 1), :] = row
    total = lax.dot_general(
        jnp.ones((SUB, LANES), jnp.float32),
        acc_ref[...],
        (((1,), (1,)), ((), ())),
        precision=lax.Precision.HIGHEST,
        preferred_element_type=jnp.float32,
    )
    for n in range(count * count // LANES):
        row = total[:1, n * LANES : (n + 1) * LANES]
        out_ref[:, n : n + 1, :] = (row + base[0][0, n : n + 1, :] if base else row)[None]


def gram(xs, rows, groups, pairs, base=None):
    count = rows * groups
    held = [xs.get(k, xs[0]) for k in range(groups)]
    extra = [] if base is None else [base]
    return pl.pallas_call(
        functools.partial(gram_kernel, rows, groups, pairs),
        out_shape=jax.ShapeDtypeStruct((1, count * count // LANES, LANES), jnp.float32),
        in_specs=[VMEM_SPEC] * (groups + len(extra)),
        out_specs=VMEM_SPEC,
        scratch_shapes=[pltpu.VMEM((count * count, LANES), jnp.float32)],
        compiler_params=pltpu.CompilerParams(vmem_limit_bytes=VMEM_LIMIT),
        cost_estimate=SHORT,
        name="gram",
    )(*map(in_vmem, held + extra))


def add_kernel(*refs):
    refs[-1][...] = sum((ref[...] for ref in refs[1:-1]), refs[0][...])


def add(blocks):
    return pl.pallas_call(
        add_kernel,
        out_shape=jax.ShapeDtypeStruct(blocks[0].shape, blocks[0].dtype),
        in_specs=[VMEM_SPEC] * len(blocks),
        out_specs=VMEM_SPEC,
        compiler_params=pltpu.CompilerParams(vmem_limit_bytes=2**21),
        cost_estimate=SHORT,
        name="add",
    )(*blocks)


def exact(left, right):
    return jnp.dot(left, right, precision=lax.Precision.HIGHEST, preferred_element_type=jnp.float32)


def weights_kernel(rows, count, width_ref, *refs):
    me = lax.axis_index("grp")
    grams, drive_ref, repel_ref = refs[:-2], refs[-2], refs[-1]

    def iota(shape, axis):
        return lax.broadcasted_iota(jnp.int32, shape, axis)

    def mask(condition):
        return jnp.where(condition, 1.0, 0.0)

    flat = sum((ref[0] for ref in grams[1:]), grams[0][0])
    lines = flat.shape[0]
    per = LANES // count
    held = exact(mask(iota((count, lines), 0) // per == iota((count, lines), 1)), flat)
    held = jnp.where(iota((count, LANES), 1) // count == iota((count, LANES), 0) % per, held, 0.0)
    inner = exact(held, mask(iota((LANES, count), 0) % count == iota((LANES, count), 1)))
    square = (count, count)
    r, c = iota(square, 0), iota(square, 1)
    order = mask(((me ^ (r // rows)) * rows + r % rows) == c)
    inner = exact(exact(order, inner), order)

    width = width_ref[0]
    diagonal = r == c
    norms = jnp.where(diagonal, inner, 0.0)
    dist = jnp.sum(norms, axis=1, keepdims=True) + jnp.sum(norms, axis=0, keepdims=True) - 2.0 * inner
    kern = jnp.exp(-dist / (width * P_SIZE))
    others = jnp.where(diagonal, 0.0, kern)
    to_drive = kern / count
    to_repel = jnp.where(diagonal, jnp.sum(others, axis=1, keepdims=True), -others) / (count * width)
    for j in range(count):
        drive_ref[j * count : (j + 1) * count, :] = jnp.broadcast_to(to_drive[:, j : j + 1], (count, LANES))
        repel_ref[j * count : (j + 1) * count, :] = jnp.broadcast_to(to_repel[:, j : j + 1], (count, LANES))


def weights(width, grams, rows, count):
    shape = jax.ShapeDtypeStruct((count * count, LANES), jnp.float32)
    return pl.pallas_call(
        functools.partial(weights_kernel, rows, count),
        out_shape=(shape, shape),
        in_specs=[SMEM_SPEC] + [VMEM_SPEC] * len(grams),
        out_specs=(VMEM_SPEC, VMEM_SPEC),
        compiler_params=pltpu.CompilerParams(vmem_limit_bytes=VMEM_LIMIT),
        cost_estimate=SHORT,
        name="weights",
    )(width, *grams)


def mix_kernel(rows, count, jobs, drive_ref, repel_ref, *refs):
    spans = [span for job in jobs for span in job[3]]
    xs, out_ref, scratch = list(refs[: len(spans)]), refs[len(spans)], refs[len(spans) + 1 :]
    offsets = [start for start, _, _ in spans]
    copies = {}
    for n, (start, size, stream) in enumerate(spans):
        if stream:
            m = len(copies)
            copies[n] = pltpu.make_async_copy(xs[n].at[pl.ds(start, size), :], scratch[m], scratch[-1].at[m])
            copies[n].start()
            xs[n], offsets[n] = scratch[m], 0
    step = SUB * rows
    done = used = 0
    for repel, dest, sources, spans in jobs:
        coef_ref = repel_ref if repel else drive_ref
        held = [(xs[n], offsets[n]) for n in range(used, used + len(sources))]
        for n in range(used, used + len(sources)):
            if n in copies:
                copies[n].wait()
        used += len(sources)
        steps = spans[0][1] // step
        wide = next(w for w in (8, 4, 2, 1) if steps % w == 0)

        def body(t, carry):
            base = pl.multiple_of(t * step * wide, step)
            sums = [[None] * rows for _ in range(wide)]
            for (ref, offset), source in zip(held, sources):
                for j in range(rows):
                    x = [ref[pl.ds(offset + base + u * step + j, SUB, stride=rows), :] for u in range(wide)]
                    for i in range(rows):
                        row = (source * rows + j) * count + dest * rows + i
                        c = jnp.broadcast_to(coef_ref[row : row + 1, :], (SUB, LANES))
                        for u in range(wide):
                            term = c * x[u]
                            sums[u][i] = term if sums[u][i] is None else sums[u][i] + term
            for u in range(wide):
                for i in range(rows):
                    out_ref[pl.ds(done + base + u * step + i, SUB, stride=rows), :] = sums[u][i]
            return carry

        lax.fori_loop(0, steps // wide, body, 0)
        done += steps * step


def mix(coefs, rows, count, jobs):
    blocks = [block for job in jobs for block in job[3]]
    streams = [block for block in blocks if block[3]]
    return pl.pallas_call(
        functools.partial(mix_kernel, rows, count, [(*job[:3], [block[1:] for block in job[3]]) for job in jobs]),
        out_shape=jax.ShapeDtypeStruct((sum(job[3][0][2] for job in jobs), LANES), jnp.float32),
        in_specs=[VMEM_SPEC] * 2 + [ANY_SPEC if block[3] else VMEM_SPEC for block in blocks],
        out_specs=VMEM_SPEC,
        scratch_shapes=[pltpu.VMEM((block[2], LANES), jnp.float32) for block in streams]
        + ([pltpu.SemaphoreType.DMA((len(streams),))] if streams else []),
        compiler_params=pltpu.CompilerParams(vmem_limit_bytes=VMEM_LIMIT),
        cost_estimate=SHORT,
        name="mix",
    )(*coefs, *[block[0] if block[3] else in_vmem(block[0]) for block in blocks])


def put_kernel(entries, part, blocks, *refs):
    me = lax.axis_index("grp")
    blocks, (out_ref, sum_ref, sems) = refs[:blocks], refs[-3:]
    copies = []
    used = 0
    for n, (parts, size, (k, row)) in enumerate(entries):
        block, start = parts[0]
        source = blocks[block].at[pl.ds(start, size), :]
        if len(parts) > 1:
            total = source[...]
            for block, start in parts[1:]:
                total = total + blocks[block][pl.ds(start, size), :]
            source = sum_ref.at[pl.ds(used, size), :]
            source[...] = total
            used += size
        offset = row if k is None else (me ^ k) * part + row
        copy = pltpu.make_async_copy(source, out_ref.at[pl.ds(offset, size), :], sems.at[n])
        copy.start()
        copies.append(copy)
    for copy in copies:
        copy.wait()


def put(entries, blocks, part, size, base=None):
    extra = [] if base is None else [base]
    moved = sum(entry[1] for entry in entries)
    scratch = sum(entry[1] for entry in entries if len(entry[0]) > 1)
    return pl.pallas_call(
        functools.partial(put_kernel, entries, part, len(blocks)),
        out_shape=jax.ShapeDtypeStruct((size, LANES), jnp.float32),
        in_specs=[VMEM_SPEC] * len(blocks) + [HBM_SPEC] * len(extra),
        out_specs=HBM_SPEC,
        scratch_shapes=[pltpu.VMEM((max(scratch, SUB), LANES), jnp.float32), pltpu.SemaphoreType.DMA((len(entries),))],
        input_output_aliases={len(blocks): 0} if extra else {},
        compiler_params=pltpu.CompilerParams(vmem_limit_bytes=VMEM_LIMIT),
        cost_estimate=pl.CostEstimate(flops=0, bytes_accessed=8 * LANES * moved, transcendentals=0),
        name="put",
    )(*blocks, *extra)


def cut_kernel(places, part, block_ref, *refs):
    me = lax.axis_index("grp")
    outs, (in_sems, out_sems) = refs[: len(places)], refs[-2:]
    through = refs[len(places) : -2]
    copies = []
    for n, (k, row, size) in enumerate(places):
        offset = row if k is None else (me ^ k) * part + row
        held = through[n] if through else outs[n]
        copies.append(pltpu.make_async_copy(block_ref.at[pl.ds(offset, size), :], held, in_sems.at[n]))
        copies[n].start()
    for copy in copies:
        copy.wait()
    moves = [pltpu.make_async_copy(held, out, out_sems.at[n]) for n, (held, out) in enumerate(zip(through, outs))]
    for move in moves:
        move.start()
    for move in moves:
        move.wait()


def cut(block, places, part, fast):
    out = pltpu.VMEM if fast else pltpu.HBM
    through = [] if fast else [pltpu.VMEM((size, LANES), jnp.float32) for _, _, size in places]
    return pl.pallas_call(
        functools.partial(cut_kernel, places, part),
        out_shape=[out((size, LANES), jnp.float32) for _, _, size in places],
        in_specs=[HBM_SPEC],
        out_specs=[VMEM_SPEC if fast else HBM_SPEC] * len(places),
        scratch_shapes=through + [pltpu.SemaphoreType.DMA((len(places),))] * 2,
        compiler_params=pltpu.CompilerParams(vmem_limit_bytes=VMEM_LIMIT),
        cost_estimate=SHORT,
        name="cut",
    )(in_hbm(block))


def shards(particles, scores, kernel_width):
    groups = lax.axis_size("grp")
    rows = particles.shape[0]
    count = rows * groups
    x, s = dense(particles), dense(scores)
    part, half = x.shape[0] // groups, x.shape[0] // 2
    near = 2 ** ((groups.bit_length() - 1) // 2)
    lows, highs = list(range(near)), list(range(0, groups, near))

    def swap(block, k, axis="grp"):
        return lax.ppermute(block, axis, [(i, i ^ k) for i in range(lax.axis_size(axis))]) if k else block

    def stages(axis):
        left, step = lax.axis_size(axis), 1
        while left > 1:
            radix = 4 if left % 4 == 0 else 2
            yield [step * k for k in range(radix)]
            left, step = left // radix, step * radix

    everyone = list(range(groups))
    direct = [k for k in everyone[1:] if k in lows or k in highs]
    distant = [k for k in everyone[1:] if k not in direct]
    size, step = x.shape[0], SUB * rows
    first = max(1, half // step * 5 // 16) * step
    split = part // step // 2 * step
    halves = [(0, split), (split, part - split)]

    def legs(k, n):
        low, high = k % near, k - k % near
        return (low, high) if n == 0 else (high, low)

    def pieces(k):
        return halves if k in distant else [(0, part)]

    order = direct + distant
    sent = cut(x, [(k, 0, part) for k in order], part, True)
    s, sent = lax.optimization_barrier((s, sent))
    bounds = [(n * half + row, length) for n in (0, 1) for row, length in ((0, first), (first, half - first))]
    s_own = cut(s, [(None, *bound) for bound in bounds], part, False)
    xs = {k: swap(block, k) for k, block in zip(order, sent)}
    xs[order[0]], x, s_own = lax.optimization_barrier((xs[order[0]], x, s_own))
    xs[0] = cut(x, [(0, 0, part)], part, True)[0]
    pairs = [(a, b) for a in everyone for b in everyone if a <= b]
    late_pairs = [pair for pair in pairs if pair[0] in distant or pair[1] in distant]
    inner = gram({k: xs[k] for k in [0] + direct}, rows, groups, [pair for pair in pairs if pair not in late_pairs])
    if late_pairs:
        inner = gram(xs, rows, groups, late_pairs, inner)
    xs = [[xs[k]] for k in everyone]

    def exchange(block, partners):
        return [swap(block, k) for k in partners]

    early = [exchange(s_own[0], lows), exchange(s_own[2], highs)]
    grams = [inner]
    pair = [s_own[1], s_own[3]]
    for partners in stages("grp"):
        total = add(grams) if len(grams) > 1 else grams[0]
        grams = [swap(total, k) for k in partners]
    early, pair, grams = lax.optimization_barrier((early, pair, grams))
    late = [exchange(pair[0], lows), exchange(pair[1], highs)]
    for partners in stages("par"):
        grams = [swap(add(grams), k, "par") for k in partners]
    coefs = weights(kernel_width, grams, rows, count)

    s = in_hbm(s)

    def send(dest, jobs, coefs):
        mixed = mix(coefs, rows, count, jobs)
        return swap(mixed, dest), lax.optimization_barrier((coefs, mixed))[0]

    def particle_jobs(dest, start, length):
        jobs = []
        for n, (row, piece) in enumerate(halves):
            begin, extent = max(start, row), min(start + length, row + piece) - max(start, row)
            if extent > 0:
                blocks = [(xs[k][n], begin - row, extent, False) if len(xs[k]) > 1 else (xs[k][0], begin, extent, False) for k in everyone]
                jobs.append((True, dest, everyone, blocks))
        return jobs

    def score_jobs(dest, n, low, high):
        jobs = []
        for held, start, end in ((early, 0, first), (late, first, half)):
            begin, extent = max(low, start), min(high, end) - max(low, start)
            if extent > 0:
                blocks = [(s, n * half + begin, extent, True)] + [(block, begin - start, extent, True) for block in held[n][1:]]
                jobs.append((False, dest, (lows, highs)[n], blocks))
        return jobs

    back, sums = {}, {}
    for k in direct:
        back[k, 0], coefs = send(k, particle_jobs(k, 0, part), coefs)
    for k in distant:
        for n in (1, 0):
            hop, coefs = send(legs(k, n)[0], particle_jobs(k, *halves[n]), coefs)
            back[k, n] = swap(hop, legs(k, n)[1])
    middle = half // step // 2 * step
    spans = [span for span in ((0, middle), (middle, half)) if span[0] < span[1]]
    for span in spans:
        for n, dests in enumerate((highs[1:], lows[1:])):
            for k in dests:
                sums[span, k], coefs = send(k, score_jobs(k, n, *span), coefs)
    own_jobs = particle_jobs(0, 0, part)
    for span in spans:
        own_jobs += score_jobs(0, 0, *span) + score_jobs(0, 1, *span)
    own = mix(coefs, rows, count, own_jobs)

    def place(k):
        return [([(n, 0)], length, (k, row)) for n, (row, length) in enumerate(pieces(k))]

    repel = put([([(0, 0)], part, (0, 0))], [own], part, size)
    for k in direct:
        repel, got = lax.optimization_barrier((repel, back[k, 0]))
        repel = put(place(k), [got], part, size, base=repel)
    drive = None
    begin = part
    for span in spans:
        length = span[1] - span[0]
        for n, dests in enumerate((highs[1:], lows[1:])):
            got = [sums[span, k] for k in dests]
            held = repel if drive is None else (drive, repel)
            held, got = lax.optimization_barrier((held, got))
            drive, repel = (None, held) if drive is None else held
            entry = ([(0, begin)] + [(1 + m, 0) for m in range(len(got))], length, (None, n * half + span[0]))
            drive = put([entry], [own, *got], part, size, base=drive)
            begin += length
    for k in distant:
        got = [back[k, n] for n in (0, 1)]
        (drive, repel), got = lax.optimization_barrier(((drive, repel), got))
        repel = put(place(k), got, part, size, base=repel)
    return (undense(drive, rows), undense(repel, rows))


def solution(mesh):
    return jax.shard_map(
        shards,
        mesh=mesh,
        in_specs=(P("grp", "par"), P("grp", "par"), P()),
        out_specs=(P("grp", "par"), P("grp", "par")),
        check_vma=False,
    )
```
